256 devices in a mesh: dp: 32 (over x, y, core), vocab: 8 (over z).
Axes of the slice: x: 4, y: 4, z: 8, core: 2. Of those that a mesh axis runs over, the one named last changes fastest.
Arguments:
- student_hidden: bfloat16 [4096, 1536], P('dp'), may hold values from -16 to 16
- head_weight: bfloat16 [1536, 32768], P('dp', 'vocab'), may hold values from -1 to 1
- teacher_logprobs: float32 [4096, 40960], P('dp', 'vocab'), may hold values from -45 to 0, as said below
- align_index: int32 [256, 2], replicated, may hold values from 0 to 319, as said below
- align_tiles: bfloat16 [256, 2, 128, 128], P('vocab'), may hold values from 0 to 6.1
- grad_scale: float32 [4096], P('dp'), may hold values from 30 to 300
Outputs:
- hidden_grad: bfloat16 [4096, 1536], P('dp', 'vocab')
- head_grad: bfloat16 [1536, 32768], P('dp', 'vocab')
The draws below stay inside these ranges and needn't reach their ends.
Inputs may be any that keep to these rules, and one draw needn't show every extreme that they name: `teacher_logprobs`: each row's exponentials sum to 1 over the 40960 teacher entries. `align_index`: teacher block j is held by vocab index j // 40. Of the 64 entries of the student blocks held by one vocab index, at most 16 name teacher blocks held by any one vocab index, and for every vocab index some vocab index holds exactly 16 of them.
All inputs are finite; a program needn't handle non-finite values.
Results may differ from the reference program's by a relative error of at most 0.015.
Values may be sent and summed in bfloat16 or wider, within the bound.
A program may use at most 128 MiB of HBM per device.

```python
import math
import jax
import jax.numpy as jnp
from jax import lax

D = 1536
BLOCK = 128
K = 2
TOK_DEV = 128
TOKENS = 4096
V_S = 32768
V_T = 40960
NBT_DEV = 40
NB_S = 256
NB_T = 320
PAIRS = 64
CAP = 16
N_DP = 32
N_VOCAB = 8


def shared_head(key):
    folded = jax.random.fold_in(key, 101)
    normal_key = jax.random.fold_in(folded, 0)
    base = jax.random.truncated_normal(normal_key, -6.0, 6.0, (D, V_S), jnp.float32)
    columns = jnp.arange(V_S)
    spread = 1.6 + 0.8 * columns.astype(jnp.float32) / V_S
    weight = jnp.clip(base * spread[None, :] / math.sqrt(D), -1.0, 1.0)
    return weight


def draw_head_weight(key, part):
    weight = shared_head(key)
    return weight.astype(jnp.bfloat16)


def draw_student_hidden(key, part):
    folded = jax.random.fold_in(key, 202)
    row_key = jax.random.fold_in(folded, 0)
    states = 0.5 * jnp.clip(jax.random.normal(row_key, (TOKENS, D), jnp.float32), -8.0, 8.0)
    return states.astype(jnp.bfloat16)


def draw_teacher_logprobs(key, part):
    folded = jax.random.fold_in(key, 303)
    value_key = jax.random.fold_in(folded, 0)
    scores = 0.7 * jax.random.truncated_normal(value_key, -6.0, 6.0, (TOKENS, V_T), jnp.float32)
    return jax.nn.log_softmax(scores, axis=1)


def draw_align_tiles(key, part):
    folded = jax.random.fold_in(key, 404)
    off_key, diag_key = jax.random.split(folded)
    level = 1.0 + 2.0 * jnp.arange(NB_S, dtype=jnp.float32) / NB_S
    off_part = jax.random.uniform(off_key, (NB_S, K, BLOCK, BLOCK), jnp.float32, 0.0, 1.0 / BLOCK)
    diagonal = jax.random.uniform(diag_key, (NB_S, K, BLOCK), jnp.float32, 0.5, 1.5)
    identity = jnp.eye(BLOCK, dtype=jnp.float32)
    tiles = level[:, None, None, None] * (off_part + diagonal[..., None] * identity)
    return tiles.astype(jnp.bfloat16)


def draw_align_index(key, part):
    folded = jax.random.fold_in(key, 505)
    offset_key, rows_key = jax.random.split(folded)
    hot_offset = jax.random.randint(offset_key, (N_VOCAB,), 0, NBT_DEV)

    def one_requester(row_key):
        pick_key, second_key, count_key, order_key, block_key = jax.random.split(row_key, 5)
        leader = jax.random.randint(pick_key, (), 0, N_VOCAB)
        runner = (leader + 1 + jax.random.randint(second_key, (), 0, N_VOCAB - 1)) % N_VOCAB
        runner_count = jax.random.randint(count_key, (), 1, min(CAP, PAIRS - CAP) + 1)
        owners = jnp.arange(N_VOCAB)
        taken = ((owners == leader) | (owners == runner)).astype(jnp.int32)
        others = jnp.argsort(taken * N_VOCAB + owners, stable=True)
        slots = jnp.arange(PAIRS)
        spread_slot = jnp.maximum(slots - CAP - runner_count, 0) % (N_VOCAB - 2)
        owner_of = jnp.where(slots < CAP, leader, jnp.where(slots < CAP + runner_count, runner, others[spread_slot]))
        owner_of = owner_of[jax.random.permutation(order_key, PAIRS)]
        uniform_block = jax.random.randint(block_key, (PAIRS,), 0, NBT_DEV)
        local_block = (uniform_block * uniform_block // NBT_DEV + hot_offset[owner_of]) % NBT_DEV
        return owner_of * NBT_DEV + local_block
    table = jax.vmap(one_requester)(jax.random.split(rows_key, N_VOCAB))
    return table.reshape(NB_S, K).astype(jnp.int32)


def steps_of(own_key, shape, pieces, low, top_value):
    def one(axis_at, shards_of):
        heights = jax.random.uniform(jax.random.fold_in(jax.random.fold_in(own_key, 6), axis_at), (shards_of,), jnp.float32, low / len(pieces), top_value / len(pieces))
        return jnp.repeat(jnp.exp(heights), shape[axis_at] // shards_of).reshape((-1,) + (1,) * (len(shape) - axis_at - 1))

    gain = one(*pieces[0])
    for cut in pieces[1:]:
        gain = gain * one(*cut)
    return gain


def setup_inputs(seed: int = 0) -> dict:
    splits = jax.random.split(jax.random.key(seed), 7)
    student_hidden = draw_student_hidden(jax.random.fold_in(splits[6], 71), 0)
    head_weight = draw_head_weight(jax.random.fold_in(splits[6], 71), 0)
    teacher_logprobs = draw_teacher_logprobs(jax.random.fold_in(splits[6], 71), 0)
    align_index = draw_align_index(jax.random.fold_in(splits[6], 71), 0)
    align_tiles = draw_align_tiles(jax.random.fold_in(splits[6], 71), 0)
    grad_scale = jnp.clip(jnp.exp(math.log(300.0) - 2.3025851 * jax.random.uniform(splits[5], (TOKENS,), jnp.float32) ** steps_of(splits[5], (TOKENS,), ((0, 32),), -0.2, 0.2)), 30.0, 300.0)
    return dict(student_hidden=student_hidden, head_weight=head_weight, teacher_logprobs=teacher_logprobs, align_index=align_index, align_tiles=align_tiles, grad_scale=grad_scale)


def reference(student_hidden, head_weight, teacher_logprobs, align_index, align_tiles, grad_scale):
    hidden_groups = student_hidden.reshape(N_DP, TOK_DEV, D)
    teacher_groups = teacher_logprobs.reshape(N_DP, TOK_DEV, V_T)
    scale_groups = grad_scale.reshape(N_DP, TOK_DEV)
    tiles_wide = align_tiles.astype(jnp.float32)
    flat_index = align_index.reshape(-1).astype(jnp.int32)

    def group_step(head_total, inputs):
        hidden_rows, teacher_rows, scale_rows = inputs
        logits = jnp.dot(hidden_rows, head_weight, preferred_element_type=jnp.float32)
        row_max = jnp.max(logits, axis=1, keepdims=True)
        shifted = jnp.exp(logits - row_max)
        row_total = jnp.sum(shifted, axis=1, keepdims=True)
        student_probs = shifted / row_total
        teacher_low = jnp.exp(teacher_rows).astype(jnp.bfloat16)
        teacher_low = lax.optimization_barrier(teacher_low)
        teacher_probs = teacher_low.astype(jnp.float32).reshape(TOK_DEV, NB_T, BLOCK)
        picked = jnp.take(teacher_probs, flat_index, axis=1).reshape(TOK_DEV, NB_S, K, BLOCK)
        mapped = jnp.einsum("tbkj,bkji->tbi", picked, tiles_wide).reshape(TOK_DEV, V_S)
        mass = jnp.sum(mapped, axis=1, keepdims=True)
        dlogits = (scale_rows[:, None] * (mass * student_probs - mapped)).astype(jnp.bfloat16)
        hidden_part = lax.dot_general(dlogits, head_weight, (((1,), (1,)), ((), ())), preferred_element_type=jnp.float32).astype(jnp.bfloat16)
        head_part = lax.dot_general(hidden_rows, dlogits, (((0,), (0,)), ((), ())), preferred_element_type=jnp.float32).astype(jnp.bfloat16)
        head_part = lax.optimization_barrier(head_part)
        return head_total + head_part.astype(jnp.float32), hidden_part

    head_total, hidden_parts = lax.scan(group_step, jnp.zeros((D, V_S), jnp.float32), (hidden_groups, teacher_groups, scale_groups))
    return hidden_parts.reshape(TOKENS, D), head_total.astype(jnp.bfloat16)
```

```python
import jax
import jax.numpy as jnp
from jax import lax
from jax.experimental import pallas as pl
from jax.experimental.pallas import tpu as pltpu
from jax.sharding import PartitionSpec as P

X, Y, C, Z = 4, 4, 2, 8
G = X * C
DP = X * Y * C
MESH = pl.DeviceIdType.MESH
F32 = jnp.float32
BF16 = jnp.bfloat16


def to_row(col):
    return jnp.transpose(jnp.broadcast_to(col, (128, 128)))[0:1, :]


def to_cols(row):
    return jnp.transpose(jnp.broadcast_to(row, (128, 128)))


def kernel(
    x_hbm, w_hbm, t_hbm, idx, tiles_hbm, gs_in,
    hg, wg,
    tl, tsend, tall, psend, prcv, x_all, x_t, w_all, e_ref, mp, tiles, dl,
    dwp, dwr, dxp, dsib, dxo, dxs, dxr, hsend, hr,
    gsb, gs_all, st1, st1r, st2, st2r, ms1, ms1r, ms2, ms2r, fin,
    sem_l, sem_t, sem_p, sem_x, sem_xf, sem_w, sem_g, sem_s1, sem_s2, sem_m1, sem_m2,
    sem_dw, sem_ds, sem_dx, sem_h,
):
    dp = lax.axis_index("dp")
    z = lax.axis_index("vocab")
    x = dp // (Y * C)
    y = (dp // C) % Y
    c = dp % C
    me = c * X + x
    D = x_hbm.shape[1]
    DR = w_hbm.shape[0]
    NB = tl.shape[1] // 128
    CG = w_all.shape[1]

    def dp_of(g):
        return ((g % X) * Y + y) * C + g // X

    sib = (x * Y + y) * C + (1 - c)

    load_t = pltpu.make_async_copy(t_hbm, tl, sem_l.at[0])
    load_t.start()
    load_x = pltpu.make_async_copy(x_hbm, x_all.at[me], sem_l.at[1])
    load_x.start()
    load_w = pltpu.make_async_copy(
        w_hbm.at[:, pl.ds(me * CG, CG)], w_all.at[pl.ds(dp * DR, DR)], sem_l.at[2]
    )
    load_w.start()
    load_tiles = pltpu.make_async_copy(
        tiles_hbm.at[pl.ds(me * 4, 4)], tiles, sem_l.at[3]
    )
    load_tiles.start()

    barrier = pltpu.get_barrier_semaphore()

    def greet_group(i, _):
        g = (me + i % G) % G
        pl.semaphore_signal(
            barrier, inc=1, device_id=(dp_of(g), (z + i // G) % Z), device_id_type=MESH
        )
        return 0

    lax.fori_loop(1, G * Z, greet_group, 0)

    def greet_plane(i, _):
        far = (dp + i) % DP

        @pl.when((far // C) % Y != y)
        def _():
            pl.semaphore_signal(barrier, inc=1, device_id=(far, z), device_id_type=MESH)

        return 0

    lax.fori_loop(1, DP, greet_plane, 0)

    gsb[...] = jnp.broadcast_to(gs_in[...], (8, 128))
    gs_all[me] = gsb[...]
    load_t.wait()

    def probs(zt, store):
        rows = jnp.exp(tl[pl.ds(zt * 16, 16), :]).astype(BF16)
        for j in range(NB):
            store(j, rows[:, j * 128 : (j + 1) * 128])

    def order(k):
        return 4 + (1 - 2 * (k % 2)) * ((k + 1) // 2)

    def t_copy(rz, src):
        zt = (z + rz) % Z
        return pltpu.make_async_remote_copy(
            src_ref=tsend.at[zt],
            dst_ref=tall.at[pl.ds(src * NB, NB)],
            send_sem=sem_t.at[0, rz],
            recv_sem=sem_t.at[1, rz],
            device_id=(dp, zt),
            device_id_type=MESH,
        )

    def prep(k, _):
        zt = (z + order(k)) % Z

        def store(j, v):
            tsend[zt, j] = v

        probs(zt, store)
        return 0

    lax.fori_loop(0, Z - 1, prep, 0)

    pl.semaphore_wait(barrier, (G * Z - 1) + (DP - G))

    def t_start(k, _):
        t_copy(order(k), z).start()
        return 0

    lax.fori_loop(0, Z - 1, t_start, 0)

    def x_copy(rx, src_g):
        return pltpu.make_async_remote_copy(
            src_ref=x_hbm,
            dst_ref=x_all.at[src_g],
            send_sem=sem_x.at[0, rx],
            recv_sem=sem_x.at[1, rx],
            device_id=(((x + rx) % X * Y + y) * C + c, z),
            device_id_type=MESH,
        )

    def xs_copy(rx, g, src):
        return pltpu.make_async_remote_copy(
            src_ref=src,
            dst_ref=x_all.at[g],
            send_sem=sem_xf.at[0, rx],
            recv_sem=sem_xf.at[1, rx],
            device_id=(sib, z),
            device_id_type=MESH,
        )

    for rx in (2, 1, 3):
        x_copy(rx, me).start()
    xs_copy(0, me, x_hbm).start()

    def g_copy(r, src_g):
        return pltpu.make_async_remote_copy(
            src_ref=gsb,
            dst_ref=gs_all.at[src_g],
            send_sem=sem_g.at[0, r],
            recv_sem=sem_g.at[1, r],
            device_id=(dp_of((me + r) % G), z),
            device_id_type=MESH,
        )

    def g_start(r, _):
        g_copy(r, me).start()
        return 0

    lax.fori_loop(1, G, g_start, 0)

    def w_copy(r, src_dp):
        far = (dp + r) % DP
        gf = (far % C) * X + far // (Y * C)
        return pltpu.make_async_remote_copy(
            src_ref=w_hbm.at[:, pl.ds(gf * CG, CG)],
            dst_ref=w_all.at[pl.ds(src_dp * DR, DR)],
            send_sem=sem_w.at[0, r],
            recv_sem=sem_w.at[1, r],
            device_id=(far, z),
            device_id_type=MESH,
        )

    def w_start(r, _):
        w_copy(r, dp).start()
        return 0

    lax.fori_loop(1, DP, w_start, 0)

    def store_own(j, v):
        tall[z * NB + j] = v

    probs(z, store_own)

    def t_wait(k, _):
        rz = order(k)
        t_copy(rz, (z + Z - rz) % Z).wait_recv()
        return 0

    lax.fori_loop(0, Z - 1, t_wait, 0)

    def p_copy(rz, rg, src_slot):
        zt = (z + rz) % Z
        g = (me + rg) % G
        return pltpu.make_async_remote_copy(
            src_ref=psend.at[zt * G + g],
            dst_ref=prcv.at[src_slot],
            send_sem=sem_p.at[0, rz * G + rg],
            recv_sem=sem_p.at[1, rz * G + rg],
            device_id=(dp_of(g), zt),
            device_id_type=MESH,
        )

    def pick(zt, g, store):
        base = zt * (G * 8) + g * 8
        for p in range(8):
            store(p, tall[idx[base + p]])

    def pick_send(i, _):
        rz = order(i // G)
        rg = i % G
        zt = (z + rz) % Z
        g = (me + rg) % G

        def store(p, v):
            psend[zt * G + g, p] = v

        pick(zt, g, store)
        p_copy(rz, rg, me * Z + z).start()
        return 0

    lax.fori_loop(0, (Z - 1) * G, pick_send, 0)

    def pick_send_here(rg, _):
        g = (me + rg) % G

        def store(p, v):
            psend[z * G + g, p] = v

        pick(z, g, store)
        p_copy(0, rg, me * Z + z).start()
        return 0

    lax.fori_loop(1, G, pick_send_here, 0)

    def store_mine(p, v):
        prcv[me * Z + z, p] = v

    pick(z, me, store_mine)

    load_x.wait()
    for rx in (1, 3, 2):
        src = c * X + (x + X - rx) % X
        x_copy(rx, src).wait_recv()
        xs_copy(rx, src, x_all.at[src]).start()

    def x_turn(r, _):
        x_t[:, pl.ds(pl.multiple_of(r * 128, 128), 128)] = jnp.transpose(x_all[r])
        return 0

    for rx in range(X):
        xs_copy(rx, (1 - c) * X + (x + X - rx) % X, x_hbm).wait_recv()
    lax.fori_loop(0, G, x_turn, 0)

    load_w.wait()

    def w_wait(r, _):
        w_copy(r, (dp + DP - r) % DP).wait_recv()
        return 0

    lax.fori_loop(1, DP, w_wait, 0)

    def logits(r, _):
        l = jnp.dot(x_all[r], w_all[...], preferred_element_type=F32)
        m = jnp.max(l, axis=1, keepdims=True)
        e = jnp.exp(l - m)
        e_ref[r] = e
        st1[0, pl.ds(r, 1), :] = to_row(m)
        st1[1, pl.ds(r, 1), :] = to_row(jnp.sum(e, axis=1, keepdims=True))
        return 0

    lax.fori_loop(0, G, logits, 0)

    def group_copy(src, dst, sems, r):
        return pltpu.make_async_remote_copy(
            src_ref=src,
            dst_ref=dst.at[r],
            send_sem=sems.at[0, r],
            recv_sem=sems.at[1, r],
            device_id=(dp_of((me + r) % G), z),
            device_id_type=MESH,
        )

    def z_copy(src, dst, sems, r):
        return pltpu.make_async_remote_copy(
            src_ref=src,
            dst_ref=dst.at[r],
            send_sem=sems.at[0, r],
            recv_sem=sems.at[1, r],
            device_id=(dp, (z + r) % Z),
            device_id_type=MESH,
        )

    def swap(copy, src, dst, sems, n):
        def start(r, _):
            copy(src, dst, sems, r).start()
            return 0

        lax.fori_loop(1, n, start, 0)

        def wait(r, _):
            copy(src, dst, sems, r).wait_recv()
            return 0

        lax.fori_loop(1, n, wait, 0)

    def merge(own, came, n, out):
        top = own[0]
        for r in range(1, n):
            top = jnp.maximum(top, came[r, 0])
        total = own[1] * jnp.exp(own[0] - top)
        for r in range(1, n):
            total = total + came[r, 1] * jnp.exp(came[r, 0] - top)
        out[0] = top
        out[1] = total

    swap(group_copy, st1, st1r, sem_s1, G)
    merge(st1, st1r, G, st2)
    swap(z_copy, st2, st2r, sem_s2, Z)
    merge(st2, st2r, Z, fin)

    def g_wait(r, _):
        g_copy(r, (me + G - r) % G).wait_recv()
        return 0

    lax.fori_loop(1, G, g_wait, 0)

    load_tiles.wait()

    def p_wait(i, _):
        rz = i // G
        rg = i % G
        p_copy(rz, rg, ((me + G - rg) % G) * Z + (z + Z - rz) % Z).wait_recv()
        return 0

    lax.fori_loop(1, G * Z, p_wait, 0)

    def mapping(r, _):
        total = jnp.zeros((128, 1), F32)
        for b in range(4):
            first = prcv[pl.ds(r * Z, Z), 2 * b].reshape(128, 128)
            second = prcv[pl.ds(r * Z, Z), 2 * b + 1].reshape(128, 128)
            m = jnp.dot(
                jnp.concatenate([first, second], axis=1), tiles[b], preferred_element_type=F32
            )
            mp[r, :, b * 128 : (b + 1) * 128] = m
            total = total + jnp.sum(m, axis=1, keepdims=True)
        ms1[pl.ds(r, 1), :] = to_row(total)
        return 0

    lax.fori_loop(0, G, mapping, 0)

    swap(group_copy, ms1, ms1r, sem_m1, G)
    mass = ms1[...]
    for r in range(1, G):
        mass = mass + ms1r[r]
    ms2[...] = mass
    swap(z_copy, ms2, ms2r, sem_m2, Z)
    mass = ms2[...]
    for r in range(1, Z):
        mass = mass + ms2r[r]
    ms1r[0] = mass * jnp.exp(st1[0] - fin[0]) / fin[1]

    def grads(r, _):
        gs_row = gs_all[r, 0:1, :]
        scale = to_cols(gs_row)
        coef = to_cols(gs_row * ms1r[0, pl.ds(r, 1), :])
        for b in range(4):
            cols = slice(b * 128, (b + 1) * 128)
            dl[pl.ds(pl.multiple_of(r * 128, 128), 128), cols] = (
                coef * e_ref[r, :, cols] - scale * mp[r, :, cols]
            ).astype(BF16)
        return 0

    lax.fori_loop(0, G, grads, 0)

    NC = D // 512
    HALF = X * 128

    def ds_copy(n):
        cols = pl.ds(pl.multiple_of(n * 512, 512), 512)
        return pltpu.make_async_remote_copy(
            src_ref=dxp.at[:, cols],
            dst_ref=dsib.at[:, cols],
            send_sem=sem_ds.at[0, n],
            recv_sem=sem_ds.at[1, n],
            device_id=(sib, z),
            device_id_type=MESH,
        )

    def dx_part(core, n):
        rows = pl.ds(pl.multiple_of(core * HALF, HALF), HALF)
        return lax.dot_general(
            dl[rows, :],
            w_all[pl.ds(pl.multiple_of(n * 512, 512), 512), :],
            (((1,), (1,)), ((), ())),
            preferred_element_type=F32,
        )

    def dx_other(n, _):
        dxp[:, pl.ds(pl.multiple_of(n * 512, 512), 512)] = dx_part(1 - c, n).astype(BF16)
        ds_copy(n).start()
        return 0

    lax.fori_loop(0, NC, dx_other, 0)

    def dx_copy(rx, n):
        cols = pl.ds(pl.multiple_of(n * 512, 512), 512)
        xt = (x + rx) % X
        return pltpu.make_async_remote_copy(
            src_ref=dxs.at[pl.ds(pl.multiple_of(xt * 128, 128), 128), cols],
            dst_ref=dxr.at[rx - 1, :, cols],
            send_sem=sem_dx.at[0, (rx - 1) * NC + n],
            recv_sem=sem_dx.at[1, (rx - 1) * NC + n],
            device_id=((xt * Y + y) * C + c, z),
            device_id_type=MESH,
        )

    def dx_mine(n, _):
        cols = pl.ds(pl.multiple_of(n * 512, 512), 512)
        dxo[:, cols] = dx_part(c, n)
        return 0

    lax.fori_loop(0, NC, dx_mine, 0)

    def dx_join(n, _):
        cols = pl.ds(pl.multiple_of(n * 512, 512), 512)
        ds_copy(n).wait_recv()
        dxs[:, cols] = (dxo[:, cols] + dsib[:, cols].astype(F32)).astype(BF16)
        for rx in (2, 1, 3):
            dx_copy(rx, n).start()
        return 0

    lax.fori_loop(0, NC, dx_join, 0)

    PER = 8
    NQ = DP // PER

    def dw_copy(far, src_y, src_g, r):
        return pltpu.make_async_remote_copy(
            src_ref=dwp.at[pl.ds(far * DR, DR)],
            dst_ref=dwr.at[src_y, :, pl.ds(src_g * CG, CG)],
            send_sem=sem_dw.at[0, r],
            recv_sem=sem_dw.at[1, r],
            device_id=(far, z),
            device_id_type=MESH,
        )

    keep_dw = pltpu.make_async_copy(
        dwp.at[pl.ds(dp * DR, DR)], dwr.at[y, :, pl.ds(me * CG, CG)], sem_l.at[4]
    )

    def dw_part(i, _):
        q = (dp // PER + 1 + i) % NQ
        rows = pl.ds(pl.multiple_of(q * (PER * DR), PER * DR), PER * DR)
        dwp[rows, :] = jnp.dot(x_t[rows, :], dl[...], preferred_element_type=F32).astype(BF16)

        def send(k, _):
            far = q * PER + (dp + k) % PER

            @pl.when(far != dp)
            def _():
                dw_copy(far, y, me, (far - dp + DP) % DP).start()

            return 0

        lax.fori_loop(0, PER, send, 0)
        return 0

    lax.fori_loop(0, NQ, dw_part, 0)
    keep_dw.start()

    def dx_wait(i, _):
        dx_copy(i // NC + 1, i % NC).wait_recv()
        return 0

    lax.fori_loop(0, (X - 1) * NC, dx_wait, 0)
    for r4 in range(4):
        own = pl.ds(pl.multiple_of(x * 128 + r4 * 32, 32), 32)
        sub = slice(r4 * 32, (r4 + 1) * 32)
        total = dxs[own, :].astype(F32)
        for k in range(X - 1):
            total = total + dxr[k, sub, :].astype(F32)
        for k in range(Z):
            hsend[k, sub, :] = total[:, k * 192 : (k + 1) * 192].astype(BF16)

    def h_copy(r):
        zt = (z + r) % Z
        return pltpu.make_async_remote_copy(
            src_ref=hsend.at[zt],
            dst_ref=hr.at[r],
            send_sem=sem_h.at[0, r],
            recv_sem=sem_h.at[1, r],
            device_id=(dp, zt),
            device_id_type=MESH,
        )

    def h_start(k, _):
        h_copy(order(k)).start()
        return 0

    lax.fori_loop(0, Z - 1, h_start, 0)

    keep_dw.wait()

    def dw_wait(r, _):
        src = (dp + DP - r) % DP
        dw_copy((dp + r) % DP, (src // C) % Y, (src % C) * X + src // (Y * C), r).wait_recv()
        return 0

    lax.fori_loop(1, DP, dw_wait, 0)

    def dw_sum(k, _):
        cols = pl.ds(pl.multiple_of(k * 512, 512), 512)
        total = dwr[0, :, cols].astype(F32)
        for k2 in range(1, Y):
            total = total + dwr[k2, :, cols].astype(F32)
        wg[:, cols] = total.astype(BF16)
        return 0

    lax.fori_loop(0, G, dw_sum, 0)

    def h_wait(r, _):
        h_copy(r).wait_recv()
        return 0

    lax.fori_loop(1, Z, h_wait, 0)
    total = hsend[z].astype(F32)
    for r in range(1, Z):
        total = total + hr[r].astype(F32)
    hg[...] = total.astype(BF16)

    def done_z(r, _):
        t_copy(r, z).wait_send()
        z_copy(st2, st2r, sem_s2, r).wait_send()
        z_copy(ms2, ms2r, sem_m2, r).wait_send()
        h_copy(r).wait_send()
        return 0

    lax.fori_loop(1, Z, done_z, 0)

    def done_g(r, _):
        g_copy(r, me).wait_send()
        group_copy(st1, st1r, sem_s1, r).wait_send()
        group_copy(ms1, ms1r, sem_m1, r).wait_send()
        return 0

    lax.fori_loop(1, G, done_g, 0)

    def done_p(i, _):
        p_copy(i // G, i % G, me * Z + z).wait_send()
        return 0

    lax.fori_loop(1, G * Z, done_p, 0)

    def done_w(r, _):
        w_copy(r, dp).wait_send()
        dw_copy((dp + r) % DP, y, me, r).wait_send()
        return 0

    lax.fori_loop(1, DP, done_w, 0)
    for rx in range(1, X):
        x_copy(rx, me).wait_send()
    for rx in range(X):
        xs_copy(rx, me, x_hbm).wait_send()

    def done_ds(n, _):
        ds_copy(n).wait_send()
        return 0

    lax.fori_loop(0, NC, done_ds, 0)

    def done_dx(i, _):
        dx_copy(i // NC + 1, i % NC).wait_send()
        return 0

    lax.fori_loop(0, (X - 1) * NC, done_dx, 0)


def body(student_hidden, head_weight, teacher_logprobs, align_index, align_tiles, grad_scale):
    T, D = student_hidden.shape
    DR, V = head_weight.shape
    VT = teacher_logprobs.shape[1]
    NB = VT // 128
    CG = V // G
    tiles = align_tiles.reshape(align_tiles.shape[0], 256, 128)
    sem = lambda n: pltpu.SemaphoreType.DMA((2, n))
    vm = pltpu.VMEM
    anywhere = pl.BlockSpec(memory_space=pl.ANY)
    in_vmem = pl.BlockSpec(memory_space=pltpu.VMEM)
    return pl.pallas_call(
        kernel,
        out_shape=(
            jax.ShapeDtypeStruct((T, D // Z), BF16),
            jax.ShapeDtypeStruct((DR, V), BF16),
        ),
        in_specs=[
            anywhere, anywhere, anywhere,
            pl.BlockSpec(memory_space=pltpu.SMEM),
            anywhere, in_vmem,
        ],
        out_specs=(in_vmem, in_vmem),
        scratch_shapes=[
            vm((T, VT), F32),
            vm((Z, NB, 16, 128), BF16),
            vm((Z * NB, 16, 128), BF16),
            vm((Z * G, 8, 16, 128), BF16),
            vm((Z * G, 8, 16, 128), BF16),
            vm((G, T, D), BF16),
            vm((D, G * T), BF16),
            vm((D, CG), BF16),
            vm((G, T, CG), F32),
            vm((G, T, CG), F32),
            vm((4, 256, 128), BF16),
            vm((G * T, CG), BF16),
            vm((D, CG), BF16),
            vm((Y, DR, V), BF16),
            vm((X * T, D), BF16),
            vm((X * T, D), BF16),
            vm((X * T, D), F32),
            vm((X * T, D), BF16),
            vm((X - 1, T, D), BF16),
            vm((Z, T, D // Z), BF16),
            vm((Z, T, D // Z), BF16),
            vm((8, 128), F32),
            vm((G, 8, 128), F32),
            vm((2, 8, 128), F32),
            vm((G, 2, 8, 128), F32),
            vm((2, 8, 128), F32),
            vm((Z, 2, 8, 128), F32),
            vm((8, 128), F32),
            vm((G, 8, 128), F32),
            vm((8, 128), F32),
            vm((Z, 8, 128), F32),
            vm((2, 8, 128), F32),
            pltpu.SemaphoreType.DMA((5,)),
            sem(Z), sem(Z * G), sem(X), sem(X), sem(DP), sem(G), sem(G), sem(Z), sem(G), sem(Z),
            sem(DP), sem(D // 512), sem((X - 1) * (D // 512)), sem(Z),
        ],
        compiler_params=pltpu.CompilerParams(
            collective_id=0, has_side_effects=True, vmem_limit_bytes=56 * 2**20
        ),
        name="distill_backward",
    )(
        student_hidden, head_weight, teacher_logprobs, align_index.reshape(-1), tiles,
        grad_scale.reshape(1, T),
    )


def solution(mesh):
    placed = (
        P("dp", None),
        P("dp", "vocab"),
        P("dp", "vocab"),
        P(),
        P("vocab", None, None, None),
        P("dp"),
    )
    return jax.shard_map(
        body,
        mesh=mesh,
        in_specs=placed,
        out_specs=(P("dp", "vocab"), P("dp", "vocab")),
        check_vma=False,
    )
```

```python
import jax
import jax.numpy as jnp
from jax import lax
from jax.experimental import pallas as pl
from jax.experimental.pallas import tpu as pltpu
from jax.sharding import PartitionSpec as P

X, Y, C, Z = 4, 4, 2, 8
G = X * C
DP = X * Y * C
MESH = pl.DeviceIdType.MESH
F32 = jnp.float32
BF16 = jnp.bfloat16


def to_row(col):
    return jnp.transpose(jnp.broadcast_to(col, (128, 128)))[0:1, :]


def to_cols(row):
    return jnp.transpose(jnp.broadcast_to(row, (128, 128)))


def kernel(
    x_hbm, w_hbm, t_hbm, idx, tiles_hbm, gs_in,
    hg, wg,
    tl, tsend, tall, psend, prcv, x_all, x_t, w_all, e_ref, tiles, dl,
    dwa, dwp, dwy, dws, dwr, dxp, dsib, dxo, dxs, dxr, hsend, hr,
    st1, st1r, st2, st2r, fin, rs_own, rs_z, rs_all, ms1, ms1r, mg, mg_all,
    sem_l, sem_t, sem_p, sem_x, sem_xf, sem_w, sem_wy, sem_s1, sem_s2, sem_r1, sem_r2, sem_m1, sem_m2,
    sem_dw, sem_dwy, sem_ds, sem_dx, sem_h,
):
    dp = lax.axis_index("dp")
    z = lax.axis_index("vocab")
    x = dp // (Y * C)
    y = (dp // C) % Y
    c = dp % C
    me = x * C + c
    D = x_hbm.shape[1]
    DR = w_hbm.shape[0]
    NB = tl.shape[1] // 128
    CG = w_all.shape[1]

    def dp_of(g):
        return ((g // C) * Y + y) * C + g % C

    sib = (x * Y + y) * C + (1 - c)

    load_t = pltpu.make_async_copy(t_hbm, tl, sem_l.at[0])
    load_t.start()
    load_x = pltpu.make_async_copy(x_hbm, x_all.at[me], sem_l.at[1])
    load_x.start()
    load_w = pltpu.make_async_copy(
        w_hbm.at[:, pl.ds(me * CG, CG)], w_all.at[pl.ds(dp * DR, DR)], sem_l.at[2]
    )
    load_w.start()
    load_tiles = pltpu.make_async_copy(
        tiles_hbm.at[pl.ds(me * 4, 4)], tiles, sem_l.at[3]
    )
    load_tiles.start()

    barrier = pltpu.get_barrier_semaphore()

    def greet_group(i, _):
        g = (me + i % G) % G
        pl.semaphore_signal(
            barrier, inc=1, device_id=(dp_of(g), (z + i // G) % Z), device_id_type=MESH
        )
        return 0

    lax.fori_loop(1, G * Z, greet_group, 0)

    for ry in range(1, Y):
        pl.semaphore_signal(
            barrier,
            inc=1,
            device_id=((x * Y + (y + ry) % Y) * C + c, z),
            device_id_type=MESH,
        )

    load_t.wait()

    def probs(zt, store):
        rows = jnp.exp(tl[pl.ds(zt * 16, 16), :]).astype(BF16)
        for j in range(NB):
            store(j, rows[:, j * 128 : (j + 1) * 128])

    def order(k):
        return 4 + (1 - 2 * (k % 2)) * ((k + 1) // 2)

    def t_copy(rz, src):
        zt = (z + rz) % Z
        return pltpu.make_async_remote_copy(
            src_ref=tsend.at[zt],
            dst_ref=tall.at[pl.ds(src * NB, NB)],
            send_sem=sem_t.at[0, rz],
            recv_sem=sem_t.at[1, rz],
            device_id=(dp, zt),
            device_id_type=MESH,
        )

    def prep(k, _):
        zt = (z + order(k)) % Z

        def store(j, v):
            tsend[zt, j] = v

        probs(zt, store)
        return 0

    lax.fori_loop(0, Z - 1, prep, 0)

    load_tiles.wait()
    ones = jnp.ones((8, 128), BF16)
    for p in range(8):
        tile = tiles[p // 2, (p % 2) * 128 : (p % 2 + 1) * 128, :]
        sums = lax.dot_general(
            ones, tile, (((1,), (1,)), ((), ())), preferred_element_type=F32
        )
        rs_own[p : p + 1, :] = sums[0:1, :]

    pl.semaphore_wait(barrier, (G * Z - 1) + (Y - 1))

    def rz_copy(r, src):
        zt = (z + r) % Z
        return pltpu.make_async_remote_copy(
            src_ref=rs_own,
            dst_ref=rs_z.at[src],
            send_sem=sem_r1.at[0, r],
            recv_sem=sem_r1.at[1, r],
            device_id=(dp, zt),
            device_id_type=MESH,
        )

    def rg_copy(r, src):
        return pltpu.make_async_remote_copy(
            src_ref=rs_z,
            dst_ref=rs_all.at[src],
            send_sem=sem_r2.at[0, r],
            recv_sem=sem_r2.at[1, r],
            device_id=(dp_of((me + r) % G), z),
            device_id_type=MESH,
        )

    def rz_start(r, _):
        rz_copy(r, z).start()
        return 0

    lax.fori_loop(1, Z, rz_start, 0)
    rs_z[z] = rs_own[...]

    def t_start(k, _):
        t_copy(order(k), z).start()
        return 0

    lax.fori_loop(0, Z - 1, t_start, 0)

    def w_copy(r, src_dp):
        g = (me + r) % G
        return pltpu.make_async_remote_copy(
            src_ref=w_hbm.at[:, pl.ds(g * CG, CG)],
            dst_ref=w_all.at[pl.ds(src_dp * DR, DR)],
            send_sem=sem_w.at[0, r],
            recv_sem=sem_w.at[1, r],
            device_id=(dp_of(g), z),
            device_id_type=MESH,
        )

    def w_start(r, _):
        w_copy(r, dp).start()
        return 0

    lax.fori_loop(1, G, w_start, 0)

    def wy_copy(i, back):
        ry = i // X + 1
        xs = i % X
        src_y = (y + Y - ry) % Y if back else y
        rows = pl.ds((xs * Y + src_y) * (C * DR), C * DR)
        return pltpu.make_async_remote_copy(
            src_ref=w_all.at[rows],
            dst_ref=w_all.at[rows],
            send_sem=sem_wy.at[0, i],
            recv_sem=sem_wy.at[1, i],
            device_id=((x * Y + (y + ry) % Y) * C + c, z),
            device_id_type=MESH,
        )

    def x_copy(rx, src_g):
        return pltpu.make_async_remote_copy(
            src_ref=x_hbm,
            dst_ref=x_all.at[src_g],
            send_sem=sem_x.at[0, rx],
            recv_sem=sem_x.at[1, rx],
            device_id=(((x + rx) % X * Y + y) * C + c, z),
            device_id_type=MESH,
        )

    def xs_copy(rx, g, src):
        return pltpu.make_async_remote_copy(
            src_ref=src,
            dst_ref=x_all.at[g],
            send_sem=sem_xf.at[0, rx],
            recv_sem=sem_xf.at[1, rx],
            device_id=(sib, z),
            device_id_type=MESH,
        )

    for rx in (2, 1, 3):
        x_copy(rx, me).start()
    xs_copy(0, me, x_hbm).start()

    def store_own(j, v):
        tall[z * NB + j] = v

    probs(z, store_own)

    def rz_wait(r, _):
        rz_copy(r, (z + Z - r) % Z).wait_recv()
        return 0

    lax.fori_loop(1, Z, rz_wait, 0)
    rs_all[me] = rs_z[...]

    def rg_start(r, _):
        rg_copy(r, me).start()
        return 0

    lax.fori_loop(1, G, rg_start, 0)

    load_w.wait()

    def w_wait(r, _):
        w_copy(r, dp_of((me + G - r) % G)).wait_recv()
        return 0

    lax.fori_loop(1, G, w_wait, 0)

    def wy_start(i, _):
        wy_copy(i, 0).start()
        return 0

    lax.fori_loop(0, (Y - 1) * X, wy_start, 0)

    load_x.wait()
    for rx in (1, 3, 2):
        src = (x + X - rx) % X * C + c
        x_copy(rx, src).wait_recv()
        xs_copy(rx, src, x_all.at[src]).start()

    def x_turn(r, _):
        x_t[:, pl.ds(pl.multiple_of(r * 128, 128), 128)] = jnp.transpose(x_all[r])
        return 0

    for rx in range(X):
        xs_copy(rx, (x + X - rx) % X * C + 1 - c, x_hbm).wait_recv()
    lax.fori_loop(0, G, x_turn, 0)

    def wy_wait(i, _):
        wy_copy(i, 1).wait_recv()
        return 0

    lax.fori_loop(0, (Y - 1) * X, wy_wait, 0)

    def logits(r, _):
        l = jnp.dot(x_all[r], w_all[...], preferred_element_type=F32)
        m = jnp.max(l, axis=1, keepdims=True)
        e = jnp.exp(l - m)
        e_ref[r] = e
        st1[0, pl.ds(r, 1), :] = to_row(m)
        st1[1, pl.ds(r, 1), :] = to_row(jnp.sum(e, axis=1, keepdims=True))
        return 0

    lax.fori_loop(0, G, logits, 0)

    def group_copy(src, dst, sems, r):
        return pltpu.make_async_remote_copy(
            src_ref=src,
            dst_ref=dst.at[r],
            send_sem=sems.at[0, r],
            recv_sem=sems.at[1, r],
            device_id=(dp_of((me + r) % G), z),
            device_id_type=MESH,
        )

    def z_copy(src, dst, sems, r):
        return pltpu.make_async_remote_copy(
            src_ref=src,
            dst_ref=dst.at[r],
            send_sem=sems.at[0, r],
            recv_sem=sems.at[1, r],
            device_id=(dp, (z + r) % Z),
            device_id_type=MESH,
        )

    def swap(copy, src, dst, sems, n):
        def start(r, _):
            copy(src, dst, sems, r).start()
            return 0

        lax.fori_loop(1, n, start, 0)

        def wait(r, _):
            copy(src, dst, sems, r).wait_recv()
            return 0

        lax.fori_loop(1, n, wait, 0)

    def merge(own, came, n, out):
        top = own[0]
        for r in range(1, n):
            top = jnp.maximum(top, came[r, 0])
        total = own[1] * jnp.exp(own[0] - top)
        for r in range(1, n):
            total = total + came[r, 1] * jnp.exp(came[r, 0] - top)
        out[0] = top
        out[1] = total

    swap(group_copy, st1, st1r, sem_s1, G)
    merge(st1, st1r, G, st2)
    def sz_start(r, _):
        z_copy(st2, st2r, sem_s2, r).start()
        return 0

    lax.fori_loop(1, Z, sz_start, 0)

    def rg_wait(r, _):
        rg_copy(r, (me + G - r) % G).wait_recv()
        return 0

    lax.fori_loop(1, G, rg_wait, 0)

    def t_wait(k, _):
        rz = order(k)
        t_copy(rz, (z + Z - rz) % Z).wait_recv()
        return 0

    lax.fori_loop(0, Z - 1, t_wait, 0)

    def p_copy(i, back):
        sign = 1 - 2 * back
        g = (x + X + sign * (i // 16 + 1)) % X * C + (c + i % 2) % C
        zt = (z + Z + sign * order(i // 2 % 8)) % Z
        return pltpu.make_async_remote_copy(
            src_ref=psend.at[zt * G + g],
            dst_ref=prcv.at[g * Z + zt if back else me * Z + z],
            send_sem=sem_p.at[0, i],
            recv_sem=sem_p.at[1, i],
            device_id=(dp_of(g), zt),
            device_id_type=MESH,
        )

    def weigh(i, acc):
        g = i % G
        zt = i // G
        for p in range(8):
            acc = acc + tall[idx[i * 8 + p]].astype(F32) * rs_all[g, zt, p : p + 1, :]
        return acc

    acc = lax.fori_loop(0, G * Z, weigh, jnp.zeros((16, 128), F32))

    own_mass = jnp.broadcast_to(jnp.sum(acc, axis=1, keepdims=True), (16, 128))
    lane = lax.broadcasted_iota(jnp.int32, (16, 128), 1)
    row = lax.broadcasted_iota(jnp.int32, (16, 128), 0)
    placed = jnp.sum(jnp.where(lane == row + z * 16, own_mass, 0.0), axis=0, keepdims=True)
    ms1[...] = jnp.broadcast_to(placed, (8, 128))

    def mz_start(r, _):
        z_copy(ms1, ms1r, sem_m1, r).start()
        return 0

    lax.fori_loop(1, Z, mz_start, 0)

    SELF = (X - 1) * 16 + 14

    def pick(i, store):
        g = (x + i // 16 + 1) % X * C + (c + i % 2) % C
        zt = (z + order(i // 2 % 8)) % Z
        base = zt * (G * 8) + g * 8
        for p in range(8):
            store(zt * G + g, p, tall[idx[base + p]])

    def pick_send(i, _):
        def store(slot, p, v):
            psend[slot, p] = v

        @pl.when(i != SELF)
        def _():
            pick(i, store)
            p_copy(i, 0).start()

        return 0

    def store_mine(slot, p, v):
        prcv[me * Z + z, p] = v

    lax.fori_loop(0, 16, pick_send, 0)
    pick(SELF, store_mine)

    def mz_wait(r, _):
        z_copy(ms1, ms1r, sem_m1, r).wait_recv()
        return 0

    lax.fori_loop(1, Z, mz_wait, 0)
    mass = ms1[...]
    for r in range(1, Z):
        mass = mass + ms1r[r]
    top_row = lax.broadcasted_iota(jnp.int32, (8, 128), 0) == 0
    mg[...] = jnp.where(top_row, mass, jnp.broadcast_to(gs_in[...], (8, 128)))

    def mg_copy(r, src):
        return pltpu.make_async_remote_copy(
            src_ref=mg,
            dst_ref=mg_all.at[src],
            send_sem=sem_m2.at[0, r],
            recv_sem=sem_m2.at[1, r],
            device_id=(dp_of((me + r) % G), z),
            device_id_type=MESH,
        )

    def mg_start(r, _):
        mg_copy(r, me).start()
        return 0

    lax.fori_loop(1, G, mg_start, 0)
    mg_all[me] = mg[...]

    lax.fori_loop(16, 32, pick_send, 0)

    def sz_wait(r, _):
        z_copy(st2, st2r, sem_s2, r).wait_recv()
        return 0

    lax.fori_loop(1, Z, sz_wait, 0)
    merge(st2, st2r, Z, fin)


    def mg_wait(r, _):
        mg_copy(r, (me + G - r) % G).wait_recv()
        return 0

    lax.fori_loop(1, G, mg_wait, 0)
    for r in range(G):
        st1r[0, 0, r : r + 1, :] = mg_all[r, 0:1, :] * mg_all[r, 1:2, :]
    fin[1] = st1r[0, 0] * jnp.exp(st1[0] - fin[0]) / fin[1]

    NC = D // 512
    PAIR = C * 128

    def ds_copy(k):
        return pltpu.make_async_remote_copy(
            src_ref=dxp.at[k],
            dst_ref=dsib.at[k],
            send_sem=sem_ds.at[0, k],
            recv_sem=sem_ds.at[1, k],
            device_id=(sib, z),
            device_id_type=MESH,
        )

    def dx_copy(k):
        return pltpu.make_async_remote_copy(
            src_ref=dxs.at[k],
            dst_ref=dxr.at[k],
            send_sem=sem_dx.at[0, k],
            recv_sem=sem_dx.at[1, k],
            device_id=(((x + X - k) % X * Y + y) * C + c, z),
            device_id_type=MESH,
        )

    def step(s):
        k = (s + 1) % X
        xs = (x + X - k) % X
        pair = pl.ds(pl.multiple_of(xs * PAIR, PAIR), PAIR)

        def p_wait(i, _):
            @pl.when(s * 16 + i != SELF)
            def _():
                p_copy(s * 16 + i, 1).wait_recv()

            return 0

        lax.fori_loop(0, 16, p_wait, 0)

        @pl.when(s + 2 < X)
        def _():
            lax.fori_loop((s + 2) * 16, (s + 3) * 16, pick_send, 0)

        for cc in range(C):
            r = xs * C + cc
            scale = to_cols(mg_all[r, 1:2, :])
            coef = to_cols(fin[1, pl.ds(r, 1), :])
            for b in range(4):
                first = prcv[pl.ds(r * Z, Z), 2 * b].reshape(128, 128)
                second = prcv[pl.ds(r * Z, Z), 2 * b + 1].reshape(128, 128)
                m = jnp.dot(
                    jnp.concatenate([first, second], axis=1),
                    tiles[b],
                    preferred_element_type=F32,
                )
                cols = slice(b * 128, (b + 1) * 128)
                dl[pl.ds(pl.multiple_of(r * 128, 128), 128), cols] = (
                    coef * e_ref[r, :, cols] - scale * m
                ).astype(BF16)
        for n in range(NC):
            cols = slice(n * 512, (n + 1) * 512)
            dxo[:, cols] = lax.dot_general(
                dl[pair, :], w_all[cols, :], (((1,), (1,)), ((), ())),
                preferred_element_type=F32,
            )
        dxp[k] = dxo[pl.ds(pl.multiple_of((1 - c) * 128, 128), 128), :].astype(BF16)
        ds_copy(k).start()

    def join(k):
        ds_copy(k).wait_recv()
        dxs[k] = (
            dxo[pl.ds(pl.multiple_of(c * 128, 128), 128), :] + dsib[k].astype(F32)
        ).astype(BF16)

    def dw_sums(k, rows):
        pair = pl.ds(pl.multiple_of((x + X - k) % X * PAIR, PAIR), PAIR)
        return jnp.dot(x_t[rows, pair], dl[pair, :], preferred_element_type=F32)

    dwa[...] = jnp.zeros_like(dwa)

    def early(i, _):
        step(i)

        def add(q, _):
            rows = pl.ds(pl.multiple_of(q * 384, 384), 384)
            dwa[rows, :] += dw_sums(i + 1, rows)
            return 0

        lax.fori_loop(0, D // 384, add, 0)
        join(i + 1)
        dx_copy(i + 1).start()
        return 0

    lax.fori_loop(0, X - 1, early, 0)
    step(X - 1)

    YR = C * DR

    def wy_rows(q, yt):
        return pl.ds((q * Y + yt) * YR, YR)

    def dwy_copy(q, ry):
        yt = (y + ry) % Y
        return pltpu.make_async_remote_copy(
            src_ref=dwp.at[wy_rows(q, yt)],
            dst_ref=dwy.at[ry - 1, q],
            send_sem=sem_dwy.at[0, ry - 1, q],
            recv_sem=sem_dwy.at[1, ry - 1, q],
            device_id=((x * Y + yt) * C + c, z),
            device_id_type=MESH,
        )

    def dw_part(i):
        q = (x + 1 + i) % X
        rows = pl.ds(pl.multiple_of(q * (Y * YR), Y * YR), Y * YR)
        total = dwa[rows, :] + dw_sums(0, rows)
        dwa[rows, :] = total
        dwp[rows, :] = total.astype(BF16)
        for ry in (2, 1, 3):
            dwy_copy(q, ry).start()

    def dw_copy(r, src_g):
        g = (me + r) % G
        return pltpu.make_async_remote_copy(
            src_ref=dws.at[g // C, pl.ds(g % C * DR, DR)],
            dst_ref=dwr.at[src_g],
            send_sem=sem_dw.at[0, r],
            recv_sem=sem_dw.at[1, r],
            device_id=(dp_of(g), z),
            device_id_type=MESH,
        )

    dw_part(0)

    join(0)

    def dx_wait(k, _):
        dx_copy(k).wait_recv()
        return 0

    lax.fori_loop(1, X, dx_wait, 0)
    for r4 in range(4):
        sub = slice(r4 * 32, (r4 + 1) * 32)
        total = dxs[0, sub, :].astype(F32)
        for k in range(1, X):
            total = total + dxr[k, sub, :].astype(F32)
        for k in range(Z):
            hsend[k, sub, :] = total[:, k * 192 : (k + 1) * 192].astype(BF16)

    def h_copy(r):
        zt = (z + r) % Z
        return pltpu.make_async_remote_copy(
            src_ref=hsend.at[zt],
            dst_ref=hr.at[r],
            send_sem=sem_h.at[0, r],
            recv_sem=sem_h.at[1, r],
            device_id=(dp, zt),
            device_id_type=MESH,
        )

    def h_start(k, _):
        h_copy(order(k)).start()
        return 0

    lax.fori_loop(0, Z - 1, h_start, 0)

    def dw_rest(i, _):
        dw_part(i)
        return 0

    lax.fori_loop(1, X, dw_rest, 0)

    def dw_join(i, _):
        q = (x + 1 + i) % X
        for ry in range(1, Y):
            dwy_copy(q, ry).wait_recv()
        total = dwa[wy_rows(q, y), :]
        for ry in range(1, Y):
            total = total + dwy[ry - 1, q].astype(F32)
        dws[q] = total.astype(BF16)
        for cc in range(C):
            r = (q * C + cc + G - me) % G

            @pl.when(r != 0)
            def _():
                dw_copy(r, me).start()

        return 0

    lax.fori_loop(0, X, dw_join, 0)
    dwr[me] = dws[x, pl.ds(pl.multiple_of(c * DR, 16), DR), :]

    def dw_wait(r, _):
        dw_copy(r, (me + G - r) % G).wait_recv()
        return 0

    lax.fori_loop(1, G, dw_wait, 0)
    for g in range(G):
        wg[:, g * CG : (g + 1) * CG] = dwr[g]

    def h_wait(r, _):
        h_copy(r).wait_recv()
        return 0

    lax.fori_loop(1, Z, h_wait, 0)
    total = hsend[z].astype(F32)
    for r in range(1, Z):
        total = total + hr[r].astype(F32)
    hg[...] = total.astype(BF16)

    def done_z(r, _):
        t_copy(r, z).wait_send()
        z_copy(st2, st2r, sem_s2, r).wait_send()
        z_copy(ms1, ms1r, sem_m1, r).wait_send()
        rz_copy(r, z).wait_send()
        h_copy(r).wait_send()
        return 0

    lax.fori_loop(1, Z, done_z, 0)

    def done_g(r, _):
        group_copy(st1, st1r, sem_s1, r).wait_send()
        rg_copy(r, me).wait_send()
        w_copy(r, dp).wait_send()
        dw_copy(r, me).wait_send()
        mg_copy(r, me).wait_send()
        return 0

    lax.fori_loop(1, G, done_g, 0)

    def done_p(i, _):
        @pl.when(i != SELF)
        def _():
            p_copy(i, 0).wait_send()

        return 0

    lax.fori_loop(0, G * Z, done_p, 0)

    def done_dw(q, _):
        for ry in range(1, Y):
            dwy_copy(q, ry).wait_send()
        return 0

    lax.fori_loop(0, X, done_dw, 0)
    for rx in range(1, X):
        x_copy(rx, me).wait_send()
    for rx in range(X):
        xs_copy(rx, me, x_hbm).wait_send()

    def done_wy(i, _):
        wy_copy(i, 0).wait_send()
        return 0

    lax.fori_loop(0, (Y - 1) * X, done_wy, 0)

    def done_ds(k, _):
        ds_copy(k).wait_send()
        return 0

    lax.fori_loop(0, X, done_ds, 0)

    def done_dx(k, _):
        dx_copy(k).wait_send()
        return 0

    lax.fori_loop(1, X, done_dx, 0)


def body(student_hidden, head_weight, teacher_logprobs, align_index, align_tiles, grad_scale):
    T, D = student_hidden.shape
    DR, V = head_weight.shape
    VT = teacher_logprobs.shape[1]
    NB = VT // 128
    CG = V // G
    tiles = align_tiles.reshape(align_tiles.shape[0], 256, 128)
    sem = lambda n: pltpu.SemaphoreType.DMA((2, n))
    vm = pltpu.VMEM
    anywhere = pl.BlockSpec(memory_space=pl.ANY)
    in_vmem = pl.BlockSpec(memory_space=pltpu.VMEM)
    return pl.pallas_call(
        kernel,
        out_shape=(
            jax.ShapeDtypeStruct((T, D // Z), BF16),
            jax.ShapeDtypeStruct((DR, V), BF16),
        ),
        in_specs=[
            anywhere, anywhere, anywhere,
            pl.BlockSpec(memory_space=pltpu.SMEM),
            anywhere, in_vmem,
        ],
        out_specs=(in_vmem, in_vmem),
        scratch_shapes=[
            vm((T, VT), F32),
            vm((Z, NB, 16, 128), BF16),
            vm((Z * NB, 16, 128), BF16),
            vm((Z * G, 8, 16, 128), BF16),
            vm((Z * G, 8, 16, 128), BF16),
            vm((G, T, D), BF16),
            vm((D, G * T), BF16),
            vm((D, CG), BF16),
            vm((G, T, CG), F32),
            vm((4, 256, 128), BF16),
            vm((G * T, CG), BF16),
            vm((D, CG), F32),
            vm((D, CG), BF16),
            vm((Y - 1, X, C * DR, CG), BF16),
            vm((X, C * DR, CG), BF16),
            vm((G, DR, CG), BF16),
            vm((X, T, D), BF16),
            vm((X, T, D), BF16),
            vm((C * T, D), F32),
            vm((X, T, D), BF16),
            vm((X, T, D), BF16),
            vm((Z, T, D // Z), BF16),
            vm((Z, T, D // Z), BF16),
            vm((2, 8, 128), F32),
            vm((G, 2, 8, 128), F32),
            vm((2, 8, 128), F32),
            vm((Z, 2, 8, 128), F32),
            vm((2, 8, 128), F32),
            vm((8, 128), F32),
            vm((Z, 8, 128), F32),
            vm((G, Z, 8, 128), F32),
            vm((8, 128), F32),
            vm((Z, 8, 128), F32),
            vm((8, 128), F32),
            vm((G, 8, 128), F32),
            pltpu.SemaphoreType.DMA((4,)),
            sem(Z), sem(Z * G), sem(X), sem(X), sem(G), sem((Y - 1) * X), sem(G), sem(Z), sem(Z), sem(G), sem(Z), sem(G),
            sem(G), pltpu.SemaphoreType.DMA((2, Y - 1, X)), sem(X), sem(X), sem(Z),
        ],
        compiler_params=pltpu.CompilerParams(
            collective_id=0, has_side_effects=True, vmem_limit_bytes=56 * 2**20
        ),
        name="distill_backward",
    )(
        student_hidden, head_weight, teacher_logprobs, align_index.reshape(-1), tiles,
        grad_scale.reshape(1, T),
    )


def solution(mesh):
    placed = (
        P("dp", None),
        P("dp", "vocab"),
        P("dp", "vocab"),
        P(),
        P("vocab", None, None, None),
        P("dp"),
    )
    return jax.shard_map(
        body,
        mesh=mesh,
        in_specs=placed,
        out_specs=(P("dp", "vocab"), P("dp", "vocab")),
        check_vma=False,
    )
```

```python
import jax
import jax.numpy as jnp
from jax import lax
from jax.experimental import pallas as pl
from jax.experimental.pallas import tpu as pltpu
from jax.sharding import PartitionSpec as P

X, Y, C, Z = 4, 4, 2, 8
K = 2
G = X * C
DP = X * Y * C
MESH = pl.DeviceIdType.MESH
F32 = jnp.float32
BF16 = jnp.bfloat16


def to_row(col):
    return jnp.transpose(jnp.broadcast_to(col, (128, 128)))[0:1, :]


def to_cols(row):
    return jnp.transpose(jnp.broadcast_to(row, (128, 128)))


def kernel(
    x_hbm, w_hbm, t_hbm, idx, tiles_hbm, gs_in,
    hg, wg,
    tl, tsend, tall, psend, prcv, x_all, x_t, w_all, e_ref, tiles, dl,
    dwa, dwp, way, way_sum, dwy, dws, dwr, dxp, dsib, dxo, dxs, dxr, hsend, hr,
    st1, st1r, st2, st2r, fin, rs_own, rs_z, rs_all, ms1, ms1r, mg, mg_all,
    sem_l, sem_t, sem_p, sem_x, sem_xf, sem_w, sem_wy, sem_s1, sem_s2, sem_r1, sem_r2, sem_m1, sem_m2,
    sem_dw, sem_dwy, sem_ds, sem_dx, sem_h,
):
    dp = lax.axis_index("dp")
    z = lax.axis_index("vocab")
    x = dp // (Y * C)
    y = (dp // C) % Y
    c = dp % C
    me = x * C + c
    D = x_hbm.shape[1]
    DR = w_hbm.shape[0]
    NB = tl.shape[1] // 128
    CG = w_all.shape[1]

    def dp_of(g):
        return ((g // C) * Y + y) * C + g % C

    sib = (x * Y + y) * C + (1 - c)

    load_t = pltpu.make_async_copy(t_hbm, tl, sem_l.at[0])
    load_t.start()
    load_x = pltpu.make_async_copy(x_hbm, x_all.at[me], sem_l.at[1])
    load_x.start()
    load_w = pltpu.make_async_copy(
        w_hbm.at[:, pl.ds(me * CG, CG)], w_all.at[pl.ds(dp * DR, DR)], sem_l.at[2]
    )
    load_w.start()
    load_tiles = pltpu.make_async_copy(
        tiles_hbm.at[pl.ds(me * 4, 4)], tiles, sem_l.at[3]
    )
    load_tiles.start()

    barrier = pltpu.get_barrier_semaphore()

    def greet_group(i, _):
        g = (me + i % G) % G
        pl.semaphore_signal(
            barrier, inc=1, device_id=(dp_of(g), (z + i // G) % Z), device_id_type=MESH
        )
        return 0

    lax.fori_loop(1, G * Z, greet_group, 0)

    for ry in range(1, Y):
        pl.semaphore_signal(
            barrier,
            inc=1,
            device_id=((x * Y + (y + ry) % Y) * C + c, z),
            device_id_type=MESH,
        )

    load_t.wait()

    def probs(zt, store):
        rows = jnp.exp(tl[pl.ds(zt * 16, 16), :]).astype(BF16)
        for j in range(NB):
            store(j, rows[:, j * 128 : (j + 1) * 128])

    def order(k):
        return 4 + (1 - 2 * (k % 2)) * ((k + 1) // 2)

    def t_copy(rz, src):
        zt = (z + rz) % Z
        return pltpu.make_async_remote_copy(
            src_ref=tsend.at[zt],
            dst_ref=tall.at[pl.ds(src * NB, NB)],
            send_sem=sem_t.at[0, rz],
            recv_sem=sem_t.at[1, rz],
            device_id=(dp, zt),
            device_id_type=MESH,
        )

    def prep(k, _):
        zt = (z + order(k)) % Z

        def store(j, v):
            tsend[zt, j] = v

        probs(zt, store)
        return 0

    lax.fori_loop(0, Z - 1, prep, 0)

    load_tiles.wait()
    ones = jnp.ones((8, 128), BF16)
    for p in range(8):
        tile = tiles[p // 2, (p % 2) * 128 : (p % 2 + 1) * 128, :]
        sums = lax.dot_general(
            ones, tile, (((1,), (1,)), ((), ())), preferred_element_type=F32
        )
        rs_own[p : p + 1, :] = sums[0:1, :]

    pl.semaphore_wait(barrier, (G * Z - 1) + (Y - 1))

    def rz_copy(r, src):
        zt = (z + r) % Z
        return pltpu.make_async_remote_copy(
            src_ref=rs_own,
            dst_ref=rs_z.at[src],
            send_sem=sem_r1.at[0, r],
            recv_sem=sem_r1.at[1, r],
            device_id=(dp, zt),
            device_id_type=MESH,
        )

    def rg_copy(r, src):
        return pltpu.make_async_remote_copy(
            src_ref=rs_z,
            dst_ref=rs_all.at[src],
            send_sem=sem_r2.at[0, r],
            recv_sem=sem_r2.at[1, r],
            device_id=(dp_of((me + r) % G), z),
            device_id_type=MESH,
        )

    def rz_start(r, _):
        rz_copy(r, z).start()
        return 0

    lax.fori_loop(1, Z, rz_start, 0)
    rs_z[z] = rs_own[...]

    def t_start(k, _):
        t_copy(order(k), z).start()
        return 0

    lax.fori_loop(0, Z - 1, t_start, 0)

    def w_copy(r, src_dp):
        g = (me + r) % G
        return pltpu.make_async_remote_copy(
            src_ref=w_hbm.at[:, pl.ds(g * CG, CG)],
            dst_ref=w_all.at[pl.ds(src_dp * DR, DR)],
            send_sem=sem_w.at[0, r],
            recv_sem=sem_w.at[1, r],
            device_id=(dp_of(g), z),
            device_id_type=MESH,
        )

    def w_start(r, _):
        w_copy(r, dp).start()
        return 0

    lax.fori_loop(1, G, w_start, 0)

    def wy_copy(i, back):
        ry = i // X + 1
        xs = i % X
        src_y = (y + Y - ry) % Y if back else y
        rows = pl.ds((xs * Y + src_y) * (C * DR), C * DR)
        return pltpu.make_async_remote_copy(
            src_ref=w_all.at[rows],
            dst_ref=w_all.at[rows],
            send_sem=sem_wy.at[0, i],
            recv_sem=sem_wy.at[1, i],
            device_id=((x * Y + (y + ry) % Y) * C + c, z),
            device_id_type=MESH,
        )

    def x_copy(rx, src_g):
        return pltpu.make_async_remote_copy(
            src_ref=x_hbm,
            dst_ref=x_all.at[src_g],
            send_sem=sem_x.at[0, rx],
            recv_sem=sem_x.at[1, rx],
            device_id=(((x + rx) % X * Y + y) * C + c, z),
            device_id_type=MESH,
        )

    def xs_copy(rx, g, src):
        return pltpu.make_async_remote_copy(
            src_ref=src,
            dst_ref=x_all.at[g],
            send_sem=sem_xf.at[0, rx],
            recv_sem=sem_xf.at[1, rx],
            device_id=(sib, z),
            device_id_type=MESH,
        )

    for rx in (2, 1, 3):
        x_copy(rx, me).start()
    xs_copy(0, me, x_hbm).start()

    def store_own(j, v):
        tall[z * NB + j] = v

    probs(z, store_own)

    def rz_wait(r, _):
        rz_copy(r, (z + Z - r) % Z).wait_recv()
        return 0

    lax.fori_loop(1, Z, rz_wait, 0)
    rs_all[me] = rs_z[...]

    def rg_start(r, _):
        rg_copy(r, me).start()
        return 0

    lax.fori_loop(1, G, rg_start, 0)

    load_w.wait()

    def w_wait(r, _):
        w_copy(r, dp_of((me + G - r) % G)).wait_recv()
        return 0

    lax.fori_loop(1, G, w_wait, 0)

    def wy_start(i, _):
        wy_copy(i, 0).start()
        return 0

    lax.fori_loop(0, (Y - 1) * X, wy_start, 0)

    load_x.wait()
    for rx in (1, 3, 2):
        src = (x + X - rx) % X * C + c
        x_copy(rx, src).wait_recv()
        xs_copy(rx, src, x_all.at[src]).start()

    def group_copy(src, dst, sems, r):
        return pltpu.make_async_remote_copy(
            src_ref=src,
            dst_ref=dst.at[r],
            send_sem=sems.at[0, r],
            recv_sem=sems.at[1, r],
            device_id=(dp_of((me + r) % G), z),
            device_id_type=MESH,
        )

    def z_copy(src, dst, sems, r):
        return pltpu.make_async_remote_copy(
            src_ref=src,
            dst_ref=dst.at[r],
            send_sem=sems.at[0, r],
            recv_sem=sems.at[1, r],
            device_id=(dp, (z + r) % Z),
            device_id_type=MESH,
        )

    def merge(own, came, n, out):
        top = own[0]
        for r in range(1, n):
            top = jnp.maximum(top, came[r, 0])
        total = own[1] * jnp.exp(own[0] - top)
        for r in range(1, n):
            total = total + came[r, 1] * jnp.exp(came[r, 0] - top)
        out[0] = top
        out[1] = total

    def rg_wait(r, _):
        rg_copy(r, (me + G - r) % G).wait_recv()
        return 0

    lax.fori_loop(1, G, rg_wait, 0)

    def t_wait(k, _):
        rz = order(k)
        t_copy(rz, (z + Z - rz) % Z).wait_recv()
        return 0

    lax.fori_loop(0, Z - 1, t_wait, 0)

    def p_copy(i, back):
        sign = 1 - 2 * back
        g = (x + X + sign * (i // 16 + 1)) % X * C + (c + i % 2) % C
        zt = (z + Z + sign * order(i // 2 % 8)) % Z
        return pltpu.make_async_remote_copy(
            src_ref=psend.at[zt * G + g],
            dst_ref=prcv.at[g * Z + zt if back else me * Z + z],
            send_sem=sem_p.at[0, i],
            recv_sem=sem_p.at[1, i],
            device_id=(dp_of(g), zt),
            device_id_type=MESH,
        )

    def weigh(i, acc):
        g = i % G
        zt = i // G
        for p in range(8):
            acc = acc + tall[idx[p % K, i * 4 + p // K]].astype(F32) * rs_all[g, zt, p : p + 1, :]
        return acc

    acc = lax.fori_loop(0, G * Z, weigh, jnp.zeros((16, 128), F32))

    own_mass = jnp.broadcast_to(jnp.sum(acc, axis=1, keepdims=True), (16, 128))
    lane = lax.broadcasted_iota(jnp.int32, (16, 128), 1)
    row = lax.broadcasted_iota(jnp.int32, (16, 128), 0)
    placed = jnp.sum(jnp.where(lane == row + z * 16, own_mass, 0.0), axis=0, keepdims=True)
    ms1[...] = jnp.broadcast_to(placed, (8, 128))

    def mz_start(r, _):
        z_copy(ms1, ms1r, sem_m1, r).start()
        return 0

    lax.fori_loop(1, Z, mz_start, 0)

    SELF = (X - 1) * 16 + 14

    def pick(i, store):
        g = (x + i // 16 + 1) % X * C + (c + i % 2) % C
        zt = (z + order(i // 2 % 8)) % Z
        base = zt * (G * 4) + g * 4
        for p in range(8):
            store(zt * G + g, p, tall[idx[p % K, base + p // K]])

    def pick_send(i, _):
        def store(slot, p, v):
            psend[slot, p] = v

        @pl.when(i != SELF)
        def _():
            pick(i, store)
            p_copy(i, 0).start()

        return 0

    def store_mine(slot, p, v):
        prcv[me * Z + z, p] = v

    lax.fori_loop(0, 8, pick_send, 0)
    pick(SELF, store_mine)

    for rx in range(X):
        xs_copy(rx, (x + X - rx) % X * C + 1 - c, x_hbm).wait_recv()

    def wy_wait(i, _):
        wy_copy(i, 1).wait_recv()
        return 0

    lax.fori_loop(0, (Y - 1) * X, wy_wait, 0)

    def logits(r, _):
        both = jnp.dot(
            x_all[pl.ds(2 * r, 2)].reshape(256, D), w_all[...], preferred_element_type=F32
        )
        for h in range(2):
            l = both[h * 128 : (h + 1) * 128]
            m = jnp.max(l, axis=1, keepdims=True)
            e = jnp.exp(l - m)
            e_ref[2 * r + h] = e
            st1[0, pl.ds(2 * r + h, 1), :] = to_row(m)
            st1[1, pl.ds(2 * r + h, 1), :] = to_row(jnp.sum(e, axis=1, keepdims=True))
        return 0

    lax.fori_loop(0, G // 2, logits, 0)

    def s_start(r, _):
        group_copy(st1, st1r, sem_s1, r).start()
        return 0

    lax.fori_loop(1, G, s_start, 0)
    lax.fori_loop(8, 16, pick_send, 0)


    def mz_wait(r, _):
        z_copy(ms1, ms1r, sem_m1, r).wait_recv()
        return 0

    lax.fori_loop(1, Z, mz_wait, 0)
    mass = ms1[...]
    for r in range(1, Z):
        mass = mass + ms1r[r]
    top_row = lax.broadcasted_iota(jnp.int32, (8, 128), 0) == 0
    mg[...] = jnp.where(top_row, mass, jnp.broadcast_to(gs_in[...], (8, 128)))

    def mg_copy(r, src):
        return pltpu.make_async_remote_copy(
            src_ref=mg,
            dst_ref=mg_all.at[src],
            send_sem=sem_m2.at[0, r],
            recv_sem=sem_m2.at[1, r],
            device_id=(dp_of((me + r) % G), z),
            device_id_type=MESH,
        )

    def mg_start(r, _):
        mg_copy(r, me).start()
        return 0

    lax.fori_loop(1, G, mg_start, 0)
    mg_all[me] = mg[...]

    def s_wait(r, _):
        group_copy(st1, st1r, sem_s1, r).wait_recv()
        return 0

    lax.fori_loop(1, G, s_wait, 0)
    merge(st1, st1r, G, st2)

    def sz_start(r, _):
        z_copy(st2, st2r, sem_s2, r).start()
        return 0

    lax.fori_loop(1, Z, sz_start, 0)
    lax.fori_loop(16, 32, pick_send, 0)

    def x_turn(r, _):
        x_t[:, pl.ds(pl.multiple_of(r * 128, 128), 128)] = jnp.transpose(x_all[r])
        return 0

    lax.fori_loop(0, G, x_turn, 0)

    def sz_wait(r, _):
        z_copy(st2, st2r, sem_s2, r).wait_recv()
        return 0

    lax.fori_loop(1, Z, sz_wait, 0)
    merge(st2, st2r, Z, fin)


    def mg_wait(r, _):
        mg_copy(r, (me + G - r) % G).wait_recv()
        return 0

    lax.fori_loop(1, G, mg_wait, 0)
    for r in range(G):
        st1r[0, 0, r : r + 1, :] = mg_all[r, 0:1, :] * mg_all[r, 1:2, :]
    fin[1] = st1r[0, 0] * jnp.exp(st1[0] - fin[0]) / fin[1]

    NC = D // 512
    PAIR = C * 128

    def ds_copy(k):
        return pltpu.make_async_remote_copy(
            src_ref=dxp.at[k],
            dst_ref=dsib.at[k],
            send_sem=sem_ds.at[0, k],
            recv_sem=sem_ds.at[1, k],
            device_id=(sib, z),
            device_id_type=MESH,
        )

    def dx_copy(k):
        return pltpu.make_async_remote_copy(
            src_ref=dxs.at[k],
            dst_ref=dxr.at[k],
            send_sem=sem_dx.at[0, k],
            recv_sem=sem_dx.at[1, k],
            device_id=(((x + X - k) % X * Y + y) * C + c, z),
            device_id_type=MESH,
        )

    def step_map(s):
        k = (s + 1) % X
        xs = (x + X - k) % X

        def p_wait(i, _):
            @pl.when(s * 16 + i != SELF)
            def _():
                p_copy(s * 16 + i, 1).wait_recv()

            return 0

        lax.fori_loop(0, 16, p_wait, 0)

        @pl.when(s + 2 < X)
        def _():
            lax.fori_loop((s + 2) * 16, (s + 3) * 16, pick_send, 0)

        for cc in range(C):
            r = xs * C + cc
            scale = to_cols(mg_all[r, 1:2, :])
            coef = to_cols(fin[1, pl.ds(r, 1), :])
            for b in range(4):
                first = prcv[pl.ds(r * Z, Z), 2 * b].reshape(128, 128)
                second = prcv[pl.ds(r * Z, Z), 2 * b + 1].reshape(128, 128)
                m = jnp.dot(
                    jnp.concatenate([first, second], axis=1),
                    tiles[b],
                    preferred_element_type=F32,
                )
                cols = slice(b * 128, (b + 1) * 128)
                dl[pl.ds(pl.multiple_of(r * 128, 128), 128), cols] = (
                    coef * e_ref[r, :, cols] - scale * m
                ).astype(BF16)

    def step_dx(s):
        k = (s + 1) % X
        pair = pl.ds(pl.multiple_of((x + X - k) % X * PAIR, PAIR), PAIR)
        for n in range(NC):
            cols = slice(n * 512, (n + 1) * 512)
            dxo[:, cols] = lax.dot_general(
                dl[pair, :], w_all[cols, :], (((1,), (1,)), ((), ())),
                preferred_element_type=F32,
            )
        dxp[k] = dxo[pl.ds(pl.multiple_of((1 - c) * 128, 128), 128), :].astype(BF16)
        ds_copy(k).start()

    def join(k):
        ds_copy(k).wait_recv()
        dxs[k] = (
            dxo[pl.ds(pl.multiple_of(c * 128, 128), 128), :] + dsib[k].astype(F32)
        ).astype(BF16)

    def dw_sums(k, rows):
        pair = pl.ds(pl.multiple_of((x + X - k) % X * PAIR, PAIR), PAIR)
        return jnp.dot(x_t[rows, pair], dl[pair, :], preferred_element_type=F32)

    dwa[...] = jnp.zeros_like(dwa)

    def early(i, _):
        step_map(i)
        step_dx(i)

        def add(q, _):
            rows = pl.ds(pl.multiple_of(q * 384, 384), 384)
            dwa[rows, :] += dw_sums(i + 1, rows)
            return 0

        lax.fori_loop(0, D // 384, add, 0)
        join(i + 1)
        dx_copy(i + 1).start()
        return 0

    lax.fori_loop(0, X - 1, early, 0)
    step_map(X - 1)

    YR = C * DR

    def next_y(d):
        return (y + 1 + d * (Y - 2)) % Y

    def to_y(d):
        return ((x * Y + next_y(d)) * C + c, z)

    def half(q, yt, h):
        return pl.ds((q * Y + yt) * YR + h * DR, DR)

    def way_copy(q, d):
        return pltpu.make_async_remote_copy(
            src_ref=dwp.at[half(q, (y + 2) % Y, d)],
            dst_ref=way.at[d, q],
            send_sem=sem_dwy.at[0, d, q],
            recv_sem=sem_dwy.at[1, d, q],
            device_id=to_y(d),
            device_id_type=MESH,
        )

    def plain_copy(q, d):
        return pltpu.make_async_remote_copy(
            src_ref=dwp.at[half(q, next_y(d), 1 - d)],
            dst_ref=dwy.at[d, q, 1 - d],
            send_sem=sem_dwy.at[0, 2 + d, q],
            recv_sem=sem_dwy.at[1, 2 + d, q],
            device_id=to_y(d),
            device_id_type=MESH,
        )

    def sum_copy(q, d):
        return pltpu.make_async_remote_copy(
            src_ref=way_sum.at[d, q],
            dst_ref=dwy.at[d, q, d],
            send_sem=sem_dwy.at[0, 4 + d, q],
            recv_sem=sem_dwy.at[1, 4 + d, q],
            device_id=to_y(d),
            device_id_type=MESH,
        )

    def dw_part(i):
        q = (x + 1 + i) % X
        rows = pl.ds(pl.multiple_of(q * (Y * YR), Y * YR), Y * YR)
        total = dwa[rows, :] + dw_sums(0, rows)
        dwa[rows, :] = total
        dwp[rows, :] = total.astype(BF16)
        for d in range(2):
            way_copy(q, d).start()
        for d in range(2):
            plain_copy(q, d).start()

    def dw_copy(r, src_g):
        g = (me + r) % G
        return pltpu.make_async_remote_copy(
            src_ref=dws.at[g // C, pl.ds(g % C * DR, DR)],
            dst_ref=dwr.at[src_g],
            send_sem=sem_dw.at[0, r],
            recv_sem=sem_dw.at[1, r],
            device_id=(dp_of(g), z),
            device_id_type=MESH,
        )

    def dw_rest(i, _):
        dw_part(i)
        return 0

    lax.fori_loop(0, 2, dw_rest, 0)
    step_dx(X - 1)
    lax.fori_loop(2, X, dw_rest, 0)

    join(0)

    def dx_wait(k, _):
        dx_copy(k).wait_recv()
        return 0

    lax.fori_loop(1, X, dx_wait, 0)
    for r4 in range(4):
        sub = slice(r4 * 32, (r4 + 1) * 32)
        total = dxs[0, sub, :].astype(F32)
        for k in range(1, X):
            total = total + dxr[k, sub, :].astype(F32)
        for k in range(Z):
            hsend[k, sub, :] = total[:, k * 192 : (k + 1) * 192].astype(BF16)

    def h_copy(r):
        zt = (z + r) % Z
        return pltpu.make_async_remote_copy(
            src_ref=hsend.at[zt],
            dst_ref=hr.at[r],
            send_sem=sem_h.at[0, r],
            recv_sem=sem_h.at[1, r],
            device_id=(dp, zt),
            device_id_type=MESH,
        )

    def h_start(k, _):
        h_copy(order(k)).start()
        return 0

    lax.fori_loop(0, Z - 1, h_start, 0)

    def dw_way(i, _):
        q = (x + 1 + i) % X
        for d in range(2):
            way_copy(q, d).wait_recv()
            way_sum[d, q] = (
                dwa[half(q, next_y(d), d), :] + way[d, q].astype(F32)
            ).astype(BF16)
            sum_copy(q, d).start()
        return 0

    lax.fori_loop(0, X, dw_way, 0)

    def dw_join(i, _):
        q = (x + 1 + i) % X
        for d in range(2):
            plain_copy(q, d).wait_recv()
            sum_copy(q, d).wait_recv()
        for h in range(2):
            total = dwa[half(q, y, h), :]
            for d in range(2):
                total = total + dwy[d, q, h].astype(F32)
            dws[q, h * DR : (h + 1) * DR, :] = total.astype(BF16)
        for cc in range(C):
            r = (q * C + cc + G - me) % G

            @pl.when(r != 0)
            def _():
                dw_copy(r, me).start()

        return 0

    lax.fori_loop(0, X, dw_join, 0)
    dwr[me] = dws[x, pl.ds(pl.multiple_of(c * DR, 16), DR), :]

    def dw_wait(r, _):
        dw_copy(r, (me + G - r) % G).wait_recv()
        return 0

    lax.fori_loop(1, G, dw_wait, 0)
    for g in range(G):
        wg[:, g * CG : (g + 1) * CG] = dwr[g]

    def h_wait(r, _):
        h_copy(r).wait_recv()
        return 0

    lax.fori_loop(1, Z, h_wait, 0)
    total = hsend[z].astype(F32)
    for r in range(1, Z):
        total = total + hr[r].astype(F32)
    hg[...] = jnp.transpose(total).astype(BF16)

    def done_z(r, _):
        t_copy(r, z).wait_send()
        z_copy(st2, st2r, sem_s2, r).wait_send()
        z_copy(ms1, ms1r, sem_m1, r).wait_send()
        rz_copy(r, z).wait_send()
        h_copy(r).wait_send()
        return 0

    lax.fori_loop(1, Z, done_z, 0)

    def done_g(r, _):
        group_copy(st1, st1r, sem_s1, r).wait_send()
        rg_copy(r, me).wait_send()
        w_copy(r, dp).wait_send()
        dw_copy(r, me).wait_send()
        mg_copy(r, me).wait_send()
        return 0

    lax.fori_loop(1, G, done_g, 0)

    def done_p(i, _):
        @pl.when(i != SELF)
        def _():
            p_copy(i, 0).wait_send()

        return 0

    lax.fori_loop(0, G * Z, done_p, 0)

    def done_dw(q, _):
        for d in range(2):
            way_copy(q, d).wait_send()
            plain_copy(q, d).wait_send()
            sum_copy(q, d).wait_send()
        return 0

    lax.fori_loop(0, X, done_dw, 0)
    for rx in range(1, X):
        x_copy(rx, me).wait_send()
    for rx in range(X):
        xs_copy(rx, me, x_hbm).wait_send()

    def done_wy(i, _):
        wy_copy(i, 0).wait_send()
        return 0

    lax.fori_loop(0, (Y - 1) * X, done_wy, 0)

    def done_ds(k, _):
        ds_copy(k).wait_send()
        return 0

    lax.fori_loop(0, X, done_ds, 0)

    def done_dx(k, _):
        dx_copy(k).wait_send()
        return 0

    lax.fori_loop(1, X, done_dx, 0)


def body(student_hidden, head_weight, teacher_logprobs, align_index, align_tiles, grad_scale):
    T, D = student_hidden.shape
    DR, V = head_weight.shape
    VT = teacher_logprobs.shape[1]
    NB = VT // 128
    CG = V // G
    tiles = align_tiles.reshape(align_tiles.shape[0], 256, 128)
    sem = lambda n: pltpu.SemaphoreType.DMA((2, n))
    vm = pltpu.VMEM
    anywhere = pl.BlockSpec(memory_space=pl.ANY)
    in_vmem = pl.BlockSpec(memory_space=pltpu.VMEM)
    hidden_grad, head_grad = pl.pallas_call(
        kernel,
        out_shape=(
            jax.ShapeDtypeStruct((D // Z, T), BF16),
            jax.ShapeDtypeStruct((DR, V), BF16),
        ),
        in_specs=[
            anywhere, anywhere, anywhere,
            pl.BlockSpec(memory_space=pltpu.SMEM),
            anywhere, in_vmem,
        ],
        out_specs=(in_vmem, in_vmem),
        scratch_shapes=[
            vm((T, VT), F32),
            vm((Z, NB, 16, 128), BF16),
            vm((Z * NB, 16, 128), BF16),
            vm((Z * G, 8, 16, 128), BF16),
            vm((Z * G, 8, 16, 128), BF16),
            vm((G, T, D), BF16),
            vm((D, G * T), BF16),
            vm((D, CG), BF16),
            vm((G, T, CG), F32),
            vm((4, 256, 128), BF16),
            vm((G * T, CG), BF16),
            vm((D, CG), F32),
            vm((D, CG), BF16),
            vm((2, X, DR, CG), BF16),
            vm((2, X, DR, CG), BF16),
            vm((2, X, 2, DR, CG), BF16),
            vm((X, C * DR, CG), BF16),
            vm((G, DR, CG), BF16),
            vm((X, T, D), BF16),
            vm((X, T, D), BF16),
            vm((C * T, D), F32),
            vm((X, T, D), BF16),
            vm((X, T, D), BF16),
            vm((Z, T, D // Z), BF16),
            vm((Z, T, D // Z), BF16),
            vm((2, 8, 128), F32),
            vm((G, 2, 8, 128), F32),
            vm((2, 8, 128), F32),
            vm((Z, 2, 8, 128), F32),
            vm((2, 8, 128), F32),
            vm((8, 128), F32),
            vm((Z, 8, 128), F32),
            vm((G, Z, 8, 128), F32),
            vm((8, 128), F32),
            vm((Z, 8, 128), F32),
            vm((8, 128), F32),
            vm((G, 8, 128), F32),
            pltpu.SemaphoreType.DMA((4,)),
            sem(Z), sem(Z * G), sem(X), sem(X), sem(G), sem((Y - 1) * X), sem(G), sem(Z), sem(Z), sem(G), sem(Z), sem(G),
            sem(G), pltpu.SemaphoreType.DMA((2, 6, X)), sem(X), sem(X), sem(Z),
        ],
        compiler_params=pltpu.CompilerParams(
            collective_id=0, has_side_effects=True, vmem_limit_bytes=56 * 2**20
        ),
        name="distill_backward",
    )(
        student_hidden, head_weight, teacher_logprobs, align_index.T, tiles,
        grad_scale.reshape(1, T),
    )
    return hidden_grad.T, head_grad


def solution(mesh):
    placed = (
        P("dp", None),
        P("dp", "vocab"),
        P("dp", "vocab"),
        P(),
        P("vocab", None, None, None),
        P("dp"),
    )
    return jax.shard_map(
        body,
        mesh=mesh,
        in_specs=placed,
        out_specs=(P("dp", "vocab"), P("dp", "vocab")),
        check_vma=False,
    )
```

```python
import jax
import jax.numpy as jnp
from jax import lax
from jax.experimental import pallas as pl
from jax.experimental.pallas import tpu as pltpu
from jax.sharding import PartitionSpec as P

X, Y, C, Z = 4, 4, 2, 8
K = 2
G = X * C
DP = X * Y * C
MESH = pl.DeviceIdType.MESH
F32 = jnp.float32
BF16 = jnp.bfloat16


def to_row(col):
    return jnp.transpose(jnp.broadcast_to(col, (128, 128)))[0:1, :]


def to_cols(row):
    return jnp.transpose(jnp.broadcast_to(row, (128, 128)))


def kernel(
    x_hbm, w_hbm, t_hbm, idx, tiles_hbm, gs_in,
    hg, wg,
    tl, tsend, tall, psend, prcv, x_all, x_t, w_all, e_ref, tiles, dl,
    dwa, dwp, way, way_sum, dwy, dws, dwr, dxp, dsib, dxo, dxs, dxr, hsend, hr,
    st1, st1r, st2, st2r, fin, rs_own, rs_z, rs_all, ms1, ms1r, mg, mg_all,
    sem_l, sem_t, sem_p, sem_x, sem_xf, sem_w, sem_wy, sem_s1, sem_s2, sem_r1, sem_r2, sem_m1, sem_m2,
    sem_dw, sem_dwy, sem_ds, sem_dx, sem_h,
):
    dp = lax.axis_index("dp")
    z = lax.axis_index("vocab")
    x = dp // (Y * C)
    y = (dp // C) % Y
    c = dp % C
    me = x * C + c
    D = x_hbm.shape[1]
    DR = w_hbm.shape[0]
    NB = tl.shape[1] // 128
    CG = w_all.shape[1]

    def dp_of(g):
        return ((g // C) * Y + y) * C + g % C

    sib = (x * Y + y) * C + (1 - c)

    load_t = pltpu.make_async_copy(t_hbm, tl, sem_l.at[0])
    load_t.start()
    load_x = pltpu.make_async_copy(x_hbm, x_all.at[me], sem_l.at[1])
    load_x.start()
    load_w = pltpu.make_async_copy(
        w_hbm.at[:, pl.ds(me * CG, CG)], w_all.at[pl.ds(dp * DR, DR)], sem_l.at[2]
    )
    load_w.start()
    load_tiles = pltpu.make_async_copy(
        tiles_hbm.at[pl.ds(me * 4, 4)], tiles, sem_l.at[3]
    )
    load_tiles.start()

    barrier = pltpu.get_barrier_semaphore()

    def greet_group(i, _):
        g = (me + i % G) % G
        pl.semaphore_signal(
            barrier, inc=1, device_id=(dp_of(g), (z + i // G) % Z), device_id_type=MESH
        )
        return 0

    lax.fori_loop(1, G * Z, greet_group, 0)

    for ry in range(1, Y):
        pl.semaphore_signal(
            barrier,
            inc=1,
            device_id=((x * Y + (y + ry) % Y) * C + c, z),
            device_id_type=MESH,
        )

    load_t.wait()

    def probs(zt, store):
        rows = jnp.exp(tl[pl.ds(zt * 16, 16), :]).astype(BF16)
        for j in range(NB):
            store(j, rows[:, j * 128 : (j + 1) * 128])

    def order(k):
        return 4 + (1 - 2 * (k % 2)) * ((k + 1) // 2)

    def t_copy(rz, src):
        zt = (z + rz) % Z
        return pltpu.make_async_remote_copy(
            src_ref=tsend.at[zt],
            dst_ref=tall.at[pl.ds(src * NB, NB)],
            send_sem=sem_t.at[0, rz],
            recv_sem=sem_t.at[1, rz],
            device_id=(dp, zt),
            device_id_type=MESH,
        )

    def prep(k, _):
        zt = (z + order(k)) % Z

        def store(j, v):
            tsend[zt, j] = v

        probs(zt, store)
        return 0

    lax.fori_loop(0, Z - 1, prep, 0)

    load_tiles.wait()
    ones = jnp.ones((8, 128), BF16)
    for p in range(8):
        tile = tiles[p // 2, (p % 2) * 128 : (p % 2 + 1) * 128, :]
        sums = lax.dot_general(
            ones, tile, (((1,), (1,)), ((), ())), preferred_element_type=F32
        )
        rs_own[p : p + 1, :] = sums[0:1, :]

    pl.semaphore_wait(barrier, (G * Z - 1) + (Y - 1))

    def rz_copy(r, src):
        zt = (z + r) % Z
        return pltpu.make_async_remote_copy(
            src_ref=rs_own,
            dst_ref=rs_z.at[src],
            send_sem=sem_r1.at[0, r],
            recv_sem=sem_r1.at[1, r],
            device_id=(dp, zt),
            device_id_type=MESH,
        )

    def rg_copy(r, src):
        return pltpu.make_async_remote_copy(
            src_ref=rs_z,
            dst_ref=rs_all.at[src],
            send_sem=sem_r2.at[0, r],
            recv_sem=sem_r2.at[1, r],
            device_id=(dp_of((me + r) % G), z),
            device_id_type=MESH,
        )

    def rz_start(r, _):
        rz_copy(r, z).start()
        return 0

    lax.fori_loop(1, Z, rz_start, 0)
    rs_z[z] = rs_own[...]

    def t_start(k, _):
        t_copy(order(k), z).start()
        return 0

    lax.fori_loop(0, Z - 1, t_start, 0)

    def w_copy(r, src_dp):
        g = (me + r) % G
        return pltpu.make_async_remote_copy(
            src_ref=w_hbm.at[:, pl.ds(g * CG, CG)],
            dst_ref=w_all.at[pl.ds(src_dp * DR, DR)],
            send_sem=sem_w.at[0, r],
            recv_sem=sem_w.at[1, r],
            device_id=(dp_of(g), z),
            device_id_type=MESH,
        )

    def w_start(r, _):
        w_copy(r, dp).start()
        return 0

    lax.fori_loop(1, G, w_start, 0)

    def wy_copy(i, back):
        ry = i // X + 1
        xs = i % X
        src_y = (y + Y - ry) % Y if back else y
        rows = pl.ds((xs * Y + src_y) * (C * DR), C * DR)
        return pltpu.make_async_remote_copy(
            src_ref=w_all.at[rows],
            dst_ref=w_all.at[rows],
            send_sem=sem_wy.at[0, i],
            recv_sem=sem_wy.at[1, i],
            device_id=((x * Y + (y + ry) % Y) * C + c, z),
            device_id_type=MESH,
        )

    def x_copy(rx, src_g):
        return pltpu.make_async_remote_copy(
            src_ref=x_hbm,
            dst_ref=x_all.at[src_g],
            send_sem=sem_x.at[0, rx],
            recv_sem=sem_x.at[1, rx],
            device_id=(((x + rx) % X * Y + y) * C + c, z),
            device_id_type=MESH,
        )

    def xs_copy(rx, g, src):
        return pltpu.make_async_remote_copy(
            src_ref=src,
            dst_ref=x_all.at[g],
            send_sem=sem_xf.at[0, rx],
            recv_sem=sem_xf.at[1, rx],
            device_id=(sib, z),
            device_id_type=MESH,
        )

    for rx in (2, 1, 3):
        x_copy(rx, me).start()
    xs_copy(0, me, x_hbm).start()

    def store_own(j, v):
        tall[z * NB + j] = v

    probs(z, store_own)

    def rz_wait(r, _):
        rz_copy(r, (z + Z - r) % Z).wait_recv()
        return 0

    lax.fori_loop(1, Z, rz_wait, 0)
    rs_all[me] = rs_z[...]

    def rg_start(r, _):
        rg_copy(r, me).start()
        return 0

    lax.fori_loop(1, G, rg_start, 0)

    load_w.wait()

    def w_wait(r, _):
        w_copy(r, dp_of((me + G - r) % G)).wait_recv()
        return 0

    lax.fori_loop(1, G, w_wait, 0)

    def wy_start(i, _):
        wy_copy(i, 0).start()
        return 0

    lax.fori_loop(0, (Y - 1) * X, wy_start, 0)

    load_x.wait()
    for rx in (1, 3, 2):
        src = (x + X - rx) % X * C + c
        x_copy(rx, src).wait_recv()
        xs_copy(rx, src, x_all.at[src]).start()

    def group_copy(src, dst, sems, r):
        return pltpu.make_async_remote_copy(
            src_ref=src,
            dst_ref=dst.at[r],
            send_sem=sems.at[0, r],
            recv_sem=sems.at[1, r],
            device_id=(dp_of((me + r) % G), z),
            device_id_type=MESH,
        )

    def z_copy(src, dst, sems, r):
        return pltpu.make_async_remote_copy(
            src_ref=src,
            dst_ref=dst.at[r],
            send_sem=sems.at[0, r],
            recv_sem=sems.at[1, r],
            device_id=(dp, (z + r) % Z),
            device_id_type=MESH,
        )

    def merge(own, came, n, out):
        top = own[0]
        for r in range(1, n):
            top = jnp.maximum(top, came[r, 0])
        total = own[1] * jnp.exp(own[0] - top)
        for r in range(1, n):
            total = total + came[r, 1] * jnp.exp(came[r, 0] - top)
        out[0] = top
        out[1] = total

    def rg_wait(r, _):
        rg_copy(r, (me + G - r) % G).wait_recv()
        return 0

    lax.fori_loop(1, G, rg_wait, 0)

    def t_wait(k, _):
        rz = order(k)
        t_copy(rz, (z + Z - rz) % Z).wait_recv()
        return 0

    lax.fori_loop(0, Z - 1, t_wait, 0)

    def p_copy(i, back):
        sign = 1 - 2 * back
        g = (x + X + sign * (i // 16 + 1)) % X * C + (c + i % 2) % C
        zt = (z + Z + sign * order(i // 2 % 8)) % Z
        return pltpu.make_async_remote_copy(
            src_ref=psend.at[zt * G + g],
            dst_ref=prcv.at[g * Z + zt if back else me * Z + z],
            send_sem=sem_p.at[0, i],
            recv_sem=sem_p.at[1, i],
            device_id=(dp_of(g), zt),
            device_id_type=MESH,
        )

    def weigh(i, acc):
        g = i % G
        zt = i // G
        for p in range(8):
            acc = acc + tall[idx[p % K, i * 4 + p // K]].astype(F32) * rs_all[g, zt, p : p + 1, :]
        return acc

    acc = lax.fori_loop(0, G * Z, weigh, jnp.zeros((16, 128), F32))

    own_mass = jnp.broadcast_to(jnp.sum(acc, axis=1, keepdims=True), (16, 128))
    lane = lax.broadcasted_iota(jnp.int32, (16, 128), 1)
    row = lax.broadcasted_iota(jnp.int32, (16, 128), 0)
    placed = jnp.sum(jnp.where(lane == row + z * 16, own_mass, 0.0), axis=0, keepdims=True)
    ms1[...] = jnp.broadcast_to(placed, (8, 128))

    def mz_start(r, _):
        z_copy(ms1, ms1r, sem_m1, r).start()
        return 0

    lax.fori_loop(1, Z, mz_start, 0)

    SELF = (X - 1) * 16 + 14

    def pick(i, store):
        g = (x + i // 16 + 1) % X * C + (c + i % 2) % C
        zt = (z + order(i // 2 % 8)) % Z
        base = zt * (G * 4) + g * 4
        for p in range(8):
            store(zt * G + g, p, tall[idx[p % K, base + p // K]])

    def pick_send(i, _):
        def store(slot, p, v):
            psend[slot, p] = v

        @pl.when(i != SELF)
        def _():
            pick(i, store)
            p_copy(i, 0).start()

        return 0

    def store_mine(slot, p, v):
        prcv[me * Z + z, p] = v

    lax.fori_loop(0, 8, pick_send, 0)
    pick(SELF, store_mine)

    for rx in range(X):
        xs_copy(rx, (x + X - rx) % X * C + 1 - c, x_hbm).wait_recv()

    def wy_wait(i, _):
        wy_copy(i, 1).wait_recv()
        return 0

    lax.fori_loop(0, (Y - 1) * X, wy_wait, 0)

    def logits(r, _):
        both = jnp.dot(
            x_all[pl.ds(2 * r, 2)].reshape(256, D), w_all[...], preferred_element_type=F32
        )
        for h in range(2):
            l = both[h * 128 : (h + 1) * 128]
            m = jnp.max(l, axis=1, keepdims=True)
            e = jnp.exp(l - m)
            e_ref[2 * r + h] = e
            st1[0, pl.ds(2 * r + h, 1), :] = to_row(m)
            st1[1, pl.ds(2 * r + h, 1), :] = to_row(jnp.sum(e, axis=1, keepdims=True))
        return 0

    lax.fori_loop(0, G // 2, logits, 0)

    def s_start(r, _):
        group_copy(st1, st1r, sem_s1, r).start()
        return 0

    lax.fori_loop(1, G, s_start, 0)
    lax.fori_loop(8, 16, pick_send, 0)


    def mz_wait(r, _):
        z_copy(ms1, ms1r, sem_m1, r).wait_recv()
        return 0

    lax.fori_loop(1, Z, mz_wait, 0)
    mass = ms1[...]
    for r in range(1, Z):
        mass = mass + ms1r[r]
    top_row = lax.broadcasted_iota(jnp.int32, (8, 128), 0) == 0
    mg[...] = jnp.where(top_row, mass, jnp.broadcast_to(gs_in[...], (8, 128)))

    def mg_copy(r, src):
        return pltpu.make_async_remote_copy(
            src_ref=mg,
            dst_ref=mg_all.at[src],
            send_sem=sem_m2.at[0, r],
            recv_sem=sem_m2.at[1, r],
            device_id=(dp_of((me + r) % G), z),
            device_id_type=MESH,
        )

    def mg_start(r, _):
        mg_copy(r, me).start()
        return 0

    lax.fori_loop(1, G, mg_start, 0)
    mg_all[me] = mg[...]

    lax.fori_loop(16, 24, pick_send, 0)

    def s_wait(r, _):
        group_copy(st1, st1r, sem_s1, r).wait_recv()
        return 0

    lax.fori_loop(1, G, s_wait, 0)
    merge(st1, st1r, G, st2)

    def sz_start(r, _):
        z_copy(st2, st2r, sem_s2, r).start()
        return 0

    lax.fori_loop(1, Z, sz_start, 0)
    lax.fori_loop(24, 32, pick_send, 0)

    def x_turn(r, _):
        x_t[:, pl.ds(pl.multiple_of(r * 128, 128), 128)] = jnp.transpose(x_all[r])
        return 0

    lax.fori_loop(0, G, x_turn, 0)

    def sz_wait(r, _):
        z_copy(st2, st2r, sem_s2, r).wait_recv()
        return 0

    lax.fori_loop(1, Z, sz_wait, 0)
    merge(st2, st2r, Z, fin)


    def mg_wait(r, _):
        mg_copy(r, (me + G - r) % G).wait_recv()
        return 0

    lax.fori_loop(1, G, mg_wait, 0)
    for r in range(G):
        st1r[0, 0, r : r + 1, :] = mg_all[r, 0:1, :] * mg_all[r, 1:2, :]
    fin[1] = st1r[0, 0] * jnp.exp(st1[0] - fin[0]) / fin[1]

    NC = D // 512
    PAIR = C * 128

    def ds_copy(k):
        return pltpu.make_async_remote_copy(
            src_ref=dxp.at[k],
            dst_ref=dsib.at[k],
            send_sem=sem_ds.at[0, k],
            recv_sem=sem_ds.at[1, k],
            device_id=(sib, z),
            device_id_type=MESH,
        )

    def dx_copy(k):
        return pltpu.make_async_remote_copy(
            src_ref=dxs.at[k],
            dst_ref=dxr.at[k],
            send_sem=sem_dx.at[0, k],
            recv_sem=sem_dx.at[1, k],
            device_id=(((x + X - k) % X * Y + y) * C + c, z),
            device_id_type=MESH,
        )

    def step_map(s):
        k = (s + 1) % X
        xs = (x + X - k) % X

        def p_wait(i, _):
            @pl.when(s * 16 + i != SELF)
            def _():
                p_copy(s * 16 + i, 1).wait_recv()

            return 0

        lax.fori_loop(0, 16, p_wait, 0)

        @pl.when(s + 2 < X)
        def _():
            lax.fori_loop((s + 2) * 16, (s + 3) * 16, pick_send, 0)

        for cc in range(C):
            r = xs * C + cc
            scale = to_cols(mg_all[r, 1:2, :])
            coef = to_cols(fin[1, pl.ds(r, 1), :])
            for b in range(4):
                first = prcv[pl.ds(r * Z, Z), 2 * b].reshape(128, 128)
                second = prcv[pl.ds(r * Z, Z), 2 * b + 1].reshape(128, 128)
                m = jnp.dot(
                    jnp.concatenate([first, second], axis=1),
                    tiles[b],
                    preferred_element_type=F32,
                )
                cols = slice(b * 128, (b + 1) * 128)
                dl[pl.ds(pl.multiple_of(r * 128, 128), 128), cols] = (
                    coef * e_ref[r, :, cols] - scale * m
                ).astype(BF16)

    def step_dx(s):
        k = (s + 1) % X
        pair = pl.ds(pl.multiple_of((x + X - k) % X * PAIR, PAIR), PAIR)
        for n in range(NC):
            cols = slice(n * 512, (n + 1) * 512)
            dxo[:, cols] = lax.dot_general(
                dl[pair, :], w_all[cols, :], (((1,), (1,)), ((), ())),
                preferred_element_type=F32,
            )
        dxp[k] = dxo[pl.ds(pl.multiple_of((1 - c) * 128, 128), 128), :].astype(BF16)
        ds_copy(k).start()

    def join(k):
        ds_copy(k).wait_recv()
        dxs[k] = (
            dxo[pl.ds(pl.multiple_of(c * 128, 128), 128), :] + dsib[k].astype(F32)
        ).astype(BF16)

    def dw_sums(k, rows):
        pair = pl.ds(pl.multiple_of((x + X - k) % X * PAIR, PAIR), PAIR)
        return jnp.dot(x_t[rows, pair], dl[pair, :], preferred_element_type=F32)

    dwa[...] = jnp.zeros_like(dwa)

    def early(i, _):
        step_map(i)
        step_dx(i)

        def add(q, _):
            rows = pl.ds(pl.multiple_of(q * 384, 384), 384)
            dwa[rows, :] += dw_sums(i + 1, rows)
            return 0

        lax.fori_loop(0, D // 384, add, 0)
        join(i + 1)
        dx_copy(i + 1).start()
        return 0

    lax.fori_loop(0, X - 1, early, 0)

    def done_8(r, _):
        t_copy(r, z).wait_send()
        z_copy(st2, st2r, sem_s2, r).wait_send()
        z_copy(ms1, ms1r, sem_m1, r).wait_send()
        rz_copy(r, z).wait_send()
        group_copy(st1, st1r, sem_s1, r).wait_send()
        rg_copy(r, me).wait_send()
        w_copy(r, dp).wait_send()
        mg_copy(r, me).wait_send()
        return 0

    lax.fori_loop(1, Z, done_8, 0)

    def done_p(i, _):
        @pl.when(i != SELF)
        def _():
            p_copy(i, 0).wait_send()

        return 0

    lax.fori_loop(0, (X - 1) * 16, done_p, 0)
    for rx in range(1, X):
        x_copy(rx, me).wait_send()
    for rx in range(X):
        xs_copy(rx, me, x_hbm).wait_send()

    def done_wy(i, _):
        wy_copy(i, 0).wait_send()
        return 0

    lax.fori_loop(0, (Y - 1) * X, done_wy, 0)
    step_map(X - 1)

    YR = C * DR

    def next_y(d):
        return (y + 1 + d * (Y - 2)) % Y

    def to_y(d):
        return ((x * Y + next_y(d)) * C + c, z)

    def half(q, yt, h):
        return pl.ds((q * Y + yt) * YR + h * DR, DR)

    def way_copy(q, d):
        return pltpu.make_async_remote_copy(
            src_ref=dwp.at[half(q, (y + 2) % Y, d)],
            dst_ref=way.at[d, q],
            send_sem=sem_dwy.at[0, d, q],
            recv_sem=sem_dwy.at[1, d, q],
            device_id=to_y(d),
            device_id_type=MESH,
        )

    def plain_copy(q, d):
        return pltpu.make_async_remote_copy(
            src_ref=dwp.at[half(q, next_y(d), 1 - d)],
            dst_ref=dwy.at[d, q, 1 - d],
            send_sem=sem_dwy.at[0, 2 + d, q],
            recv_sem=sem_dwy.at[1, 2 + d, q],
            device_id=to_y(d),
            device_id_type=MESH,
        )

    def sum_copy(q, d):
        return pltpu.make_async_remote_copy(
            src_ref=way_sum.at[d, q],
            dst_ref=dwy.at[d, q, d],
            send_sem=sem_dwy.at[0, 4 + d, q],
            recv_sem=sem_dwy.at[1, 4 + d, q],
            device_id=to_y(d),
            device_id_type=MESH,
        )

    def dw_part(i):
        q = (x + 1 + i) % X
        rows = pl.ds(pl.multiple_of(q * (Y * YR), Y * YR), Y * YR)
        total = dwa[rows, :] + dw_sums(0, rows)
        dwa[rows, :] = total
        dwp[rows, :] = total.astype(BF16)
        for d in range(2):
            way_copy(q, d).start()
        for d in range(2):
            plain_copy(q, d).start()

    def dw_copy(r, src_g):
        g = (me + r) % G
        return pltpu.make_async_remote_copy(
            src_ref=dws.at[g // C, pl.ds(g % C * DR, DR)],
            dst_ref=dwr.at[src_g],
            send_sem=sem_dw.at[0, r],
            recv_sem=sem_dw.at[1, r],
            device_id=(dp_of(g), z),
            device_id_type=MESH,
        )

    def dw_rest(i, _):
        dw_part(i)
        return 0

    lax.fori_loop(0, 2, dw_rest, 0)
    step_dx(X - 1)
    lax.fori_loop(2, X, dw_rest, 0)

    join(0)

    def dx_wait(k, _):
        dx_copy(k).wait_recv()
        return 0

    lax.fori_loop(1, X, dx_wait, 0)
    for r4 in range(4):
        sub = slice(r4 * 32, (r4 + 1) * 32)
        total = dxs[0, sub, :].astype(F32)
        for k in range(1, X):
            total = total + dxr[k, sub, :].astype(F32)
        for k in range(Z):
            hsend[k, sub, :] = total[:, k * 192 : (k + 1) * 192].astype(BF16)

    def h_copy(r):
        zt = (z + r) % Z
        return pltpu.make_async_remote_copy(
            src_ref=hsend.at[zt],
            dst_ref=hr.at[r],
            send_sem=sem_h.at[0, r],
            recv_sem=sem_h.at[1, r],
            device_id=(dp, zt),
            device_id_type=MESH,
        )

    def h_start(k, _):
        h_copy(order(k)).start()
        return 0

    lax.fori_loop(0, Z - 1, h_start, 0)
    lax.fori_loop((X - 1) * 16, G * Z, done_p, 0)

    def done_dx(k, _):
        dx_copy(k).wait_send()
        ds_copy(k).wait_send()
        return 0

    lax.fori_loop(1, X, done_dx, 0)
    ds_copy(0).wait_send()

    def dw_way(i, _):
        q = (x + 1 + i) % X
        for d in range(2):
            way_copy(q, d).wait_recv()
            way_sum[d, q] = (
                dwa[half(q, next_y(d), d), :] + way[d, q].astype(F32)
            ).astype(BF16)
            sum_copy(q, d).start()
        return 0

    lax.fori_loop(0, X, dw_way, 0)

    def dw_join(i, _):
        q = (x + 1 + i) % X
        for d in range(2):
            plain_copy(q, d).wait_recv()
            sum_copy(q, d).wait_recv()
        for h in range(2):
            total = dwa[half(q, y, h), :]
            for d in range(2):
                total = total + dwy[d, q, h].astype(F32)
            dws[q, h * DR : (h + 1) * DR, :] = total.astype(BF16)
        for cc in range(C):
            r = (q * C + cc + G - me) % G

            @pl.when(r != 0)
            def _():
                dw_copy(r, me).start()

        return 0

    lax.fori_loop(0, X, dw_join, 0)
    dwr[me] = dws[x, pl.ds(pl.multiple_of(c * DR, 16), DR), :]

    def dw_wait(r, _):
        dw_copy(r, (me + G - r) % G).wait_recv()
        return 0

    lax.fori_loop(1, G, dw_wait, 0)
    for g in range(G):
        wg[:, g * CG : (g + 1) * CG] = dwr[g]

    def h_wait(r, _):
        h_copy(r).wait_recv()
        return 0

    lax.fori_loop(1, Z, h_wait, 0)
    total = hsend[z].astype(F32)
    for r in range(1, Z):
        total = total + hr[r].astype(F32)
    hg[...] = jnp.transpose(total).astype(BF16)

    def done_h(r, _):
        h_copy(r).wait_send()
        dw_copy(r, me).wait_send()
        return 0

    lax.fori_loop(1, Z, done_h, 0)

    def done_dw(q, _):
        for d in range(2):
            way_copy(q, d).wait_send()
            plain_copy(q, d).wait_send()
            sum_copy(q, d).wait_send()
        return 0

    lax.fori_loop(0, X, done_dw, 0)


def body(student_hidden, head_weight, teacher_logprobs, align_index, align_tiles, grad_scale):
    T, D = student_hidden.shape
    DR, V = head_weight.shape
    VT = teacher_logprobs.shape[1]
    NB = VT // 128
    CG = V // G
    tiles = align_tiles.reshape(align_tiles.shape[0], 256, 128)
    sem = lambda n: pltpu.SemaphoreType.DMA((2, n))
    vm = pltpu.VMEM
    anywhere = pl.BlockSpec(memory_space=pl.ANY)
    in_vmem = pl.BlockSpec(memory_space=pltpu.VMEM)
    hidden_grad, head_grad = pl.pallas_call(
        kernel,
        out_shape=(
            jax.ShapeDtypeStruct((D // Z, T), BF16),
            jax.ShapeDtypeStruct((DR, V), BF16),
        ),
        in_specs=[
            anywhere, anywhere, anywhere,
            pl.BlockSpec(memory_space=pltpu.SMEM),
            anywhere, in_vmem,
        ],
        out_specs=(in_vmem, in_vmem),
        scratch_shapes=[
            vm((T, VT), F32),
            vm((Z, NB, 16, 128), BF16),
            vm((Z * NB, 16, 128), BF16),
            vm((Z * G, 8, 16, 128), BF16),
            vm((Z * G, 8, 16, 128), BF16),
            vm((G, T, D), BF16),
            vm((D, G * T), BF16),
            vm((D, CG), BF16),
            vm((G, T, CG), F32),
            vm((4, 256, 128), BF16),
            vm((G * T, CG), BF16),
            vm((D, CG), F32),
            vm((D, CG), BF16),
            vm((2, X, DR, CG), BF16),
            vm((2, X, DR, CG), BF16),
            vm((2, X, 2, DR, CG), BF16),
            vm((X, C * DR, CG), BF16),
            vm((G, DR, CG), BF16),
            vm((X, T, D), BF16),
            vm((X, T, D), BF16),
            vm((C * T, D), F32),
            vm((X, T, D), BF16),
            vm((X, T, D), BF16),
            vm((Z, T, D // Z), BF16),
            vm((Z, T, D // Z), BF16),
            vm((2, 8, 128), F32),
            vm((G, 2, 8, 128), F32),
            vm((2, 8, 128), F32),
            vm((Z, 2, 8, 128), F32),
            vm((2, 8, 128), F32),
            vm((8, 128), F32),
            vm((Z, 8, 128), F32),
            vm((G, Z, 8, 128), F32),
            vm((8, 128), F32),
            vm((Z, 8, 128), F32),
            vm((8, 128), F32),
            vm((G, 8, 128), F32),
            pltpu.SemaphoreType.DMA((4,)),
            sem(Z), sem(Z * G), sem(X), sem(X), sem(G), sem((Y - 1) * X), sem(G), sem(Z), sem(Z), sem(G), sem(Z), sem(G),
            sem(G), pltpu.SemaphoreType.DMA((2, 6, X)), sem(X), sem(X), sem(Z),
        ],
        compiler_params=pltpu.CompilerParams(
            collective_id=0, has_side_effects=True, vmem_limit_bytes=56 * 2**20
        ),
        name="distill_backward",
    )(
        student_hidden, head_weight, teacher_logprobs, align_index.T, tiles,
        grad_scale.reshape(1, T),
    )
    return hidden_grad.T, head_grad


def solution(mesh):
    placed = (
        P("dp", None),
        P("dp", "vocab"),
        P("dp", "vocab"),
        P(),
        P("vocab", None, None, None),
        P("dp"),
    )
    return jax.shard_map(
        body,
        mesh=mesh,
        in_specs=placed,
        out_specs=(P("dp", "vocab"), P("dp", "vocab")),
        check_vma=False,
    )
```

```python
import jax
import jax.numpy as jnp
from jax import lax
from jax.experimental import pallas as pl
from jax.experimental.pallas import tpu as pltpu
from jax.sharding import PartitionSpec as P

X, Y, C, Z = 4, 4, 2, 8
K = 2
G = X * C
DP = X * Y * C
MESH = pl.DeviceIdType.MESH
F32 = jnp.float32
BF16 = jnp.bfloat16


def to_row(col):
    return jnp.transpose(jnp.broadcast_to(col, (128, 128)))[0:1, :]


def to_cols(row):
    return jnp.transpose(jnp.broadcast_to(row, (128, 128)))


def kernel(
    x_hbm, w_hbm, t_hbm, idx, tiles_hbm, gs_in,
    hg, wg,
    tl, tsend, tall, psend, prcv, x_all, x_t, w_all, e_ref, tiles, dl,
    dwa, dwp, way, way_sum, dwy, dws, dwr, dxp, dsib, dxo, dxs, dxr, hsend, hr,
    st1, st1r, st2, st2r, fin, rs_own, rs_z, rs_all, ms1, ms1r, mg, mg_all,
    sem_l, sem_t, sem_p, sem_x, sem_xf, sem_w, sem_wy, sem_s1, sem_s2, sem_r1, sem_r2, sem_m1, sem_m2,
    sem_dw, sem_dwy, sem_ds, sem_dx, sem_h,
):
    dp = lax.axis_index("dp")
    z = lax.axis_index("vocab")
    x = dp // (Y * C)
    y = (dp // C) % Y
    c = dp % C
    me = x * C + c
    D = x_hbm.shape[1]
    DR = w_hbm.shape[0]
    NB = tl.shape[1] // 128
    CG = w_all.shape[1]

    def dp_of(g):
        return ((g // C) * Y + y) * C + g % C

    sib = (x * Y + y) * C + (1 - c)

    load_t = pltpu.make_async_copy(t_hbm, tl, sem_l.at[0])
    load_t.start()
    load_x = pltpu.make_async_copy(x_hbm, x_all.at[me], sem_l.at[1])
    load_x.start()
    load_w = pltpu.make_async_copy(
        w_hbm.at[:, pl.ds(me * CG, CG)], w_all.at[pl.ds(dp * DR, DR)], sem_l.at[2]
    )
    load_w.start()
    load_tiles = pltpu.make_async_copy(
        tiles_hbm.at[pl.ds(me * 4, 4)], tiles, sem_l.at[3]
    )
    load_tiles.start()

    barrier = pltpu.get_barrier_semaphore()

    def greet_group(i, _):
        g = (me + i % G) % G
        pl.semaphore_signal(
            barrier, inc=1, device_id=(dp_of(g), (z + i // G) % Z), device_id_type=MESH
        )
        return 0

    lax.fori_loop(1, G * Z, greet_group, 0)

    for ry in range(1, Y):
        pl.semaphore_signal(
            barrier,
            inc=1,
            device_id=((x * Y + (y + ry) % Y) * C + c, z),
            device_id_type=MESH,
        )

    load_t.wait()

    def probs(zt, store):
        rows = jnp.exp(tl[pl.ds(zt * 16, 16), :]).astype(BF16)
        for j in range(NB):
            store(j, rows[:, j * 128 : (j + 1) * 128])

    def order(k):
        return 4 + (1 - 2 * (k % 2)) * ((k + 1) // 2)

    def t_copy(rz, src):
        zt = (z + rz) % Z
        return pltpu.make_async_remote_copy(
            src_ref=tsend.at[zt],
            dst_ref=tall.at[pl.ds(src * NB, NB)],
            send_sem=sem_t.at[0, rz],
            recv_sem=sem_t.at[1, rz],
            device_id=(dp, zt),
            device_id_type=MESH,
        )

    def prep(k, _):
        zt = (z + order(k)) % Z

        def store(j, v):
            tsend[zt, j] = v

        probs(zt, store)
        return 0

    lax.fori_loop(0, Z - 1, prep, 0)

    load_tiles.wait()
    ones = jnp.ones((8, 128), BF16)
    for p in range(8):
        tile = tiles[p // 2, (p % 2) * 128 : (p % 2 + 1) * 128, :]
        sums = lax.dot_general(
            ones, tile, (((1,), (1,)), ((), ())), preferred_element_type=F32
        )
        rs_own[p : p + 1, :] = sums[0:1, :]

    pl.semaphore_wait(barrier, (G * Z - 1) + (Y - 1))

    def rz_copy(r, src):
        zt = (z + r) % Z
        return pltpu.make_async_remote_copy(
            src_ref=rs_own,
            dst_ref=rs_z.at[src],
            send_sem=sem_r1.at[0, r],
            recv_sem=sem_r1.at[1, r],
            device_id=(dp, zt),
            device_id_type=MESH,
        )

    def rg_copy(r, src):
        return pltpu.make_async_remote_copy(
            src_ref=rs_z,
            dst_ref=rs_all.at[src],
            send_sem=sem_r2.at[0, r],
            recv_sem=sem_r2.at[1, r],
            device_id=(dp_of((me + r) % G), z),
            device_id_type=MESH,
        )

    def rz_start(r, _):
        rz_copy(r, z).start()
        return 0

    lax.fori_loop(1, Z, rz_start, 0)
    rs_z[z] = rs_own[...]

    def t_start(k, _):
        t_copy(order(k), z).start()
        return 0

    lax.fori_loop(0, Z - 1, t_start, 0)

    def w_copy(r, src_dp):
        g = (me + r) % G
        return pltpu.make_async_remote_copy(
            src_ref=w_hbm.at[:, pl.ds(g * CG, CG)],
            dst_ref=w_all.at[pl.ds(src_dp * DR, DR)],
            send_sem=sem_w.at[0, r],
            recv_sem=sem_w.at[1, r],
            device_id=(dp_of(g), z),
            device_id_type=MESH,
        )

    def w_start(r, _):
        w_copy(r, dp).start()
        return 0

    lax.fori_loop(1, G, w_start, 0)

    def wy_copy(i, back):
        ry = i // X + 1
        xs = i % X
        src_y = (y + Y - ry) % Y if back else y
        rows = pl.ds((xs * Y + src_y) * (C * DR), C * DR)
        return pltpu.make_async_remote_copy(
            src_ref=w_all.at[rows],
            dst_ref=w_all.at[rows],
            send_sem=sem_wy.at[0, i],
            recv_sem=sem_wy.at[1, i],
            device_id=((x * Y + (y + ry) % Y) * C + c, z),
            device_id_type=MESH,
        )

    def x_copy(rx, src_g):
        return pltpu.make_async_remote_copy(
            src_ref=x_hbm,
            dst_ref=x_all.at[src_g],
            send_sem=sem_x.at[0, rx],
            recv_sem=sem_x.at[1, rx],
            device_id=(((x + rx) % X * Y + y) * C + c, z),
            device_id_type=MESH,
        )

    def xs_copy(rx, g, src):
        return pltpu.make_async_remote_copy(
            src_ref=src,
            dst_ref=x_all.at[g],
            send_sem=sem_xf.at[0, rx],
            recv_sem=sem_xf.at[1, rx],
            device_id=(sib, z),
            device_id_type=MESH,
        )

    for rx in (2, 1, 3):
        x_copy(rx, me).start()
    xs_copy(0, me, x_hbm).start()

    def store_own(j, v):
        tall[z * NB + j] = v

    probs(z, store_own)

    def rz_wait(r, _):
        rz_copy(r, (z + Z - r) % Z).wait_recv()
        return 0

    lax.fori_loop(1, Z, rz_wait, 0)
    rs_all[me] = rs_z[...]

    def rg_start(r, _):
        rg_copy(r, me).start()
        return 0

    lax.fori_loop(1, G, rg_start, 0)

    load_w.wait()

    def w_wait(r, _):
        w_copy(r, dp_of((me + G - r) % G)).wait_recv()
        return 0

    lax.fori_loop(1, G, w_wait, 0)

    def wy_start(i, _):
        wy_copy(i, 0).start()
        return 0

    lax.fori_loop(0, (Y - 1) * X, wy_start, 0)

    load_x.wait()
    for rx in (1, 3, 2):
        src = (x + X - rx) % X * C + c
        x_copy(rx, src).wait_recv()
        xs_copy(rx, src, x_all.at[src]).start()

    def group_copy(src, dst, sems, r):
        return pltpu.make_async_remote_copy(
            src_ref=src,
            dst_ref=dst.at[r],
            send_sem=sems.at[0, r],
            recv_sem=sems.at[1, r],
            device_id=(dp_of((me + r) % G), z),
            device_id_type=MESH,
        )

    def z_copy(src, dst, sems, r):
        return pltpu.make_async_remote_copy(
            src_ref=src,
            dst_ref=dst.at[r],
            send_sem=sems.at[0, r],
            recv_sem=sems.at[1, r],
            device_id=(dp, (z + r) % Z),
            device_id_type=MESH,
        )

    def merge(own, came, n, out):
        top = own[0]
        for r in range(1, n):
            top = jnp.maximum(top, came[r, 0])
        total = own[1] * jnp.exp(own[0] - top)
        for r in range(1, n):
            total = total + came[r, 1] * jnp.exp(came[r, 0] - top)
        out[0] = top
        out[1] = total

    def rg_wait(r, _):
        rg_copy(r, (me + G - r) % G).wait_recv()
        return 0

    lax.fori_loop(1, G, rg_wait, 0)

    def t_wait(k, _):
        rz = order(k)
        t_copy(rz, (z + Z - rz) % Z).wait_recv()
        return 0

    lax.fori_loop(0, Z - 1, t_wait, 0)

    def p_copy(i, back):
        sign = 1 - 2 * back
        g = (x + X + sign * (i // 16 + 1)) % X * C + (c + i % 2) % C
        zt = (z + Z + sign * order(i // 2 % 8)) % Z
        return pltpu.make_async_remote_copy(
            src_ref=psend.at[zt * G + g],
            dst_ref=prcv.at[g * Z + zt if back else me * Z + z],
            send_sem=sem_p.at[0, i],
            recv_sem=sem_p.at[1, i],
            device_id=(dp_of(g), zt),
            device_id_type=MESH,
        )

    def weigh(i, acc):
        g = i % G
        zt = i // G
        for p in range(8):
            acc = acc + tall[idx[p % K, i * 4 + p // K]].astype(F32) * rs_all[g, zt, p : p + 1, :]
        return acc

    acc = lax.fori_loop(0, G * Z, weigh, jnp.zeros((16, 128), F32))

    own_mass = jnp.broadcast_to(jnp.sum(acc, axis=1, keepdims=True), (16, 128))
    lane = lax.broadcasted_iota(jnp.int32, (16, 128), 1)
    row = lax.broadcasted_iota(jnp.int32, (16, 128), 0)
    placed = jnp.sum(jnp.where(lane == row + z * 16, own_mass, 0.0), axis=0, keepdims=True)
    ms1[...] = jnp.broadcast_to(placed, (8, 128))

    def mz_start(r, _):
        z_copy(ms1, ms1r, sem_m1, r).start()
        return 0

    lax.fori_loop(1, Z, mz_start, 0)

    SELF = (X - 1) * 16 + 14

    def pick(i, store):
        g = (x + i // 16 + 1) % X * C + (c + i % 2) % C
        zt = (z + order(i // 2 % 8)) % Z
        base = zt * (G * 4) + g * 4
        for p in range(8):
            store(zt * G + g, p, tall[idx[p % K, base + p // K]])

    def pick_send(i, _):
        def store(slot, p, v):
            psend[slot, p] = v

        @pl.when(i != SELF)
        def _():
            pick(i, store)
            p_copy(i, 0).start()

        return 0

    def store_mine(slot, p, v):
        prcv[me * Z + z, p] = v

    lax.fori_loop(0, 8, pick_send, 0)
    pick(SELF, store_mine)

    for rx in range(X):
        xs_copy(rx, (x + X - rx) % X * C + 1 - c, x_hbm).wait_recv()

    def wy_wait(i, _):
        wy_copy(i, 1).wait_recv()
        return 0

    lax.fori_loop(0, (Y - 1) * X, wy_wait, 0)

    def logits(r, _):
        both = jnp.dot(
            x_all[pl.ds(2 * r, 2)].reshape(256, D), w_all[...], preferred_element_type=F32
        )
        for h in range(2):
            l = both[h * 128 : (h + 1) * 128]
            m = jnp.max(l, axis=1, keepdims=True)
            e = jnp.exp(l - m)
            e_ref[2 * r + h] = e
            st1[0, pl.ds(2 * r + h, 1), :] = to_row(m)
            st1[1, pl.ds(2 * r + h, 1), :] = to_row(jnp.sum(e, axis=1, keepdims=True))
        return 0

    lax.fori_loop(0, G // 2, logits, 0)

    def s_start(r, _):
        group_copy(st1, st1r, sem_s1, r).start()
        return 0

    lax.fori_loop(1, G, s_start, 0)
    lax.fori_loop(8, 16, pick_send, 0)


    def mz_wait(r, _):
        z_copy(ms1, ms1r, sem_m1, r).wait_recv()
        return 0

    lax.fori_loop(1, Z, mz_wait, 0)
    mass = ms1[...]
    for r in range(1, Z):
        mass = mass + ms1r[r]
    top_row = lax.broadcasted_iota(jnp.int32, (8, 128), 0) == 0
    mg[...] = jnp.where(top_row, mass, jnp.broadcast_to(gs_in[...], (8, 128)))

    def mg_copy(r, src):
        return pltpu.make_async_remote_copy(
            src_ref=mg,
            dst_ref=mg_all.at[src],
            send_sem=sem_m2.at[0, r],
            recv_sem=sem_m2.at[1, r],
            device_id=(dp_of((me + r) % G), z),
            device_id_type=MESH,
        )

    def mg_start(r, _):
        mg_copy(r, me).start()
        return 0

    lax.fori_loop(1, G, mg_start, 0)
    mg_all[me] = mg[...]

    lax.fori_loop(16, 24, pick_send, 0)

    def x_turn(r, _):
        x_t[:, pl.ds(pl.multiple_of(r * 128, 128), 128)] = jnp.transpose(x_all[r])
        return 0

    lax.fori_loop(0, G, x_turn, 0)

    def s_wait(r, _):
        group_copy(st1, st1r, sem_s1, r).wait_recv()
        return 0

    lax.fori_loop(1, G, s_wait, 0)
    merge(st1, st1r, G, st2)

    def sz_start(r, _):
        z_copy(st2, st2r, sem_s2, r).start()
        return 0

    lax.fori_loop(1, Z, sz_start, 0)
    lax.fori_loop(24, 32, pick_send, 0)


    def sz_wait(r, _):
        z_copy(st2, st2r, sem_s2, r).wait_recv()
        return 0

    lax.fori_loop(1, Z, sz_wait, 0)
    merge(st2, st2r, Z, fin)


    def mg_wait(r, _):
        mg_copy(r, (me + G - r) % G).wait_recv()
        return 0

    lax.fori_loop(1, G, mg_wait, 0)
    for r in range(G):
        st1r[0, 0, r : r + 1, :] = mg_all[r, 0:1, :] * mg_all[r, 1:2, :]
    fin[1] = st1r[0, 0] * jnp.exp(st1[0] - fin[0]) / fin[1]

    NC = D // 512
    PAIR = C * 128

    def ds_copy(k):
        return pltpu.make_async_remote_copy(
            src_ref=dxp.at[k],
            dst_ref=dsib.at[k],
            send_sem=sem_ds.at[0, k],
            recv_sem=sem_ds.at[1, k],
            device_id=(sib, z),
            device_id_type=MESH,
        )

    def dx_copy(k):
        return pltpu.make_async_remote_copy(
            src_ref=dxs.at[k],
            dst_ref=dxr.at[k],
            send_sem=sem_dx.at[0, k],
            recv_sem=sem_dx.at[1, k],
            device_id=(((x + X - k) % X * Y + y) * C + c, z),
            device_id_type=MESH,
        )

    def step_map(s):
        k = (s + 1) % X
        xs = (x + X - k) % X

        def p_wait(i, _):
            @pl.when(s * 16 + i != SELF)
            def _():
                p_copy(s * 16 + i, 1).wait_recv()

            return 0

        lax.fori_loop(0, 16, p_wait, 0)

        @pl.when(s + 2 < X)
        def _():
            lax.fori_loop((s + 2) * 16, (s + 3) * 16, pick_send, 0)

        for cc in range(C):
            r = xs * C + cc
            scale = to_cols(mg_all[r, 1:2, :])
            coef = to_cols(fin[1, pl.ds(r, 1), :])
            for b in range(4):
                first = prcv[pl.ds(r * Z, Z), 2 * b].reshape(128, 128)
                second = prcv[pl.ds(r * Z, Z), 2 * b + 1].reshape(128, 128)
                m = jnp.dot(
                    jnp.concatenate([first, second], axis=1),
                    tiles[b],
                    preferred_element_type=F32,
                )
                cols = slice(b * 128, (b + 1) * 128)
                dl[pl.ds(pl.multiple_of(r * 128, 128), 128), cols] = (
                    coef * e_ref[r, :, cols] - scale * m
                ).astype(BF16)

    def step_dx(s):
        k = (s + 1) % X
        pair = pl.ds(pl.multiple_of((x + X - k) % X * PAIR, PAIR), PAIR)
        for n in range(NC):
            cols = slice(n * 512, (n + 1) * 512)
            dxo[:, cols] = lax.dot_general(
                dl[pair, :], w_all[cols, :], (((1,), (1,)), ((), ())),
                preferred_element_type=F32,
            )
        dxp[k] = dxo[pl.ds(pl.multiple_of((1 - c) * 128, 128), 128), :].astype(BF16)
        ds_copy(k).start()

    def join(k):
        ds_copy(k).wait_recv()
        dxs[k] = (
            dxo[pl.ds(pl.multiple_of(c * 128, 128), 128), :] + dsib[k].astype(F32)
        ).astype(BF16)

    def dw_sums(k, rows):
        pair = pl.ds(pl.multiple_of((x + X - k) % X * PAIR, PAIR), PAIR)
        return jnp.dot(x_t[rows, pair], dl[pair, :], preferred_element_type=F32)

    dwa[...] = jnp.zeros_like(dwa)

    def early(i, _):
        step_map(i)
        step_dx(i)

        def add(q, _):
            rows = pl.ds(pl.multiple_of(q * 384, 384), 384)
            dwa[rows, :] += dw_sums(i + 1, rows)
            return 0

        lax.fori_loop(0, D // 384, add, 0)
        join(i + 1)
        dx_copy(i + 1).start()
        return 0

    lax.fori_loop(0, X - 1, early, 0)

    def done_8(r, _):
        t_copy(r, z).wait_send()
        z_copy(st2, st2r, sem_s2, r).wait_send()
        z_copy(ms1, ms1r, sem_m1, r).wait_send()
        rz_copy(r, z).wait_send()
        group_copy(st1, st1r, sem_s1, r).wait_send()
        rg_copy(r, me).wait_send()
        w_copy(r, dp).wait_send()
        mg_copy(r, me).wait_send()
        return 0

    lax.fori_loop(1, Z, done_8, 0)

    def done_p(i, _):
        @pl.when(i != SELF)
        def _():
            p_copy(i, 0).wait_send()

        return 0

    lax.fori_loop(0, (X - 1) * 16, done_p, 0)
    for rx in range(1, X):
        x_copy(rx, me).wait_send()
    for rx in range(X):
        xs_copy(rx, me, x_hbm).wait_send()

    def done_wy(i, _):
        wy_copy(i, 0).wait_send()
        return 0

    lax.fori_loop(0, (Y - 1) * X, done_wy, 0)
    step_map(X - 1)

    YR = C * DR

    def next_y(d):
        return (y + 1 + d * (Y - 2)) % Y

    def to_y(d):
        return ((x * Y + next_y(d)) * C + c, z)

    def half(q, yt, h):
        return pl.ds((q * Y + yt) * YR + h * DR, DR)

    def way_copy(q, d):
        return pltpu.make_async_remote_copy(
            src_ref=dwp.at[half(q, (y + 2) % Y, d)],
            dst_ref=way.at[d, q],
            send_sem=sem_dwy.at[0, d, q],
            recv_sem=sem_dwy.at[1, d, q],
            device_id=to_y(d),
            device_id_type=MESH,
        )

    def plain_copy(q, d):
        return pltpu.make_async_remote_copy(
            src_ref=dwp.at[half(q, next_y(d), 1 - d)],
            dst_ref=dwy.at[d, q, 1 - d],
            send_sem=sem_dwy.at[0, 2 + d, q],
            recv_sem=sem_dwy.at[1, 2 + d, q],
            device_id=to_y(d),
            device_id_type=MESH,
        )

    def sum_copy(q, d):
        return pltpu.make_async_remote_copy(
            src_ref=way_sum.at[d, q],
            dst_ref=dwy.at[d, q, d],
            send_sem=sem_dwy.at[0, 4 + d, q],
            recv_sem=sem_dwy.at[1, 4 + d, q],
            device_id=to_y(d),
            device_id_type=MESH,
        )

    def dw_part(i):
        q = (x + 1 + i) % X
        rows = pl.ds(pl.multiple_of(q * (Y * YR), Y * YR), Y * YR)
        total = dwa[rows, :] + dw_sums(0, rows)
        dwa[rows, :] = total
        dwp[rows, :] = total.astype(BF16)
        for d in range(2):
            way_copy(q, d).start()
        for d in range(2):
            plain_copy(q, d).start()

    def dw_copy(r, src_g):
        g = (me + r) % G
        return pltpu.make_async_remote_copy(
            src_ref=dws.at[g // C, pl.ds(g % C * DR, DR)],
            dst_ref=dwr.at[src_g],
            send_sem=sem_dw.at[0, r],
            recv_sem=sem_dw.at[1, r],
            device_id=(dp_of(g), z),
            device_id_type=MESH,
        )

    def dw_rest(i, _):
        dw_part(i)
        return 0

    lax.fori_loop(0, 2, dw_rest, 0)
    step_dx(X - 1)
    lax.fori_loop(2, X, dw_rest, 0)

    join(0)

    def dx_wait(k, _):
        dx_copy(k).wait_recv()
        return 0

    lax.fori_loop(1, X, dx_wait, 0)
    for r4 in range(4):
        sub = slice(r4 * 32, (r4 + 1) * 32)
        total = dxs[0, sub, :].astype(F32)
        for k in range(1, X):
            total = total + dxr[k, sub, :].astype(F32)
        for k in range(Z):
            hsend[k, sub, :] = total[:, k * 192 : (k + 1) * 192].astype(BF16)

    def h_copy(r):
        zt = (z + r) % Z
        return pltpu.make_async_remote_copy(
            src_ref=hsend.at[zt],
            dst_ref=hr.at[r],
            send_sem=sem_h.at[0, r],
            recv_sem=sem_h.at[1, r],
            device_id=(dp, zt),
            device_id_type=MESH,
        )

    def h_start(k, _):
        h_copy(order(k)).start()
        return 0

    lax.fori_loop(0, Z - 1, h_start, 0)
    lax.fori_loop((X - 1) * 16, G * Z, done_p, 0)

    def done_dx(k, _):
        dx_copy(k).wait_send()
        ds_copy(k).wait_send()
        return 0

    lax.fori_loop(1, X, done_dx, 0)
    ds_copy(0).wait_send()

    def dw_way(i, _):
        q = (x + 1 + i) % X
        for d in range(2):
            way_copy(q, d).wait_recv()
            way_sum[d, q] = (
                dwa[half(q, next_y(d), d), :] + way[d, q].astype(F32)
            ).astype(BF16)
            sum_copy(q, d).start()
        return 0

    lax.fori_loop(0, X, dw_way, 0)

    def dw_join(i, _):
        q = (x + 1 + i) % X
        for d in range(2):
            plain_copy(q, d).wait_recv()
            sum_copy(q, d).wait_recv()
        for h in range(2):
            total = dwa[half(q, y, h), :]
            for d in range(2):
                total = total + dwy[d, q, h].astype(F32)
            dws[q, h * DR : (h + 1) * DR, :] = total.astype(BF16)
        for cc in range(C):
            r = (q * C + cc + G - me) % G

            @pl.when(r != 0)
            def _():
                dw_copy(r, me).start()

        return 0

    lax.fori_loop(0, X, dw_join, 0)
    dwr[me] = dws[x, pl.ds(pl.multiple_of(c * DR, 16), DR), :]

    def dw_wait(r, _):
        dw_copy(r, (me + G - r) % G).wait_recv()
        return 0

    lax.fori_loop(1, G, dw_wait, 0)
    for g in range(G):
        wg[:, g * CG : (g + 1) * CG] = dwr[g]

    def h_wait(r, _):
        h_copy(r).wait_recv()
        return 0

    lax.fori_loop(1, Z, h_wait, 0)
    total = hsend[z].astype(F32)
    for r in range(1, Z):
        total = total + hr[r].astype(F32)
    hg[...] = jnp.transpose(total).astype(BF16)

    def done_h(r, _):
        h_copy(r).wait_send()
        dw_copy(r, me).wait_send()
        return 0

    lax.fori_loop(1, Z, done_h, 0)

    def done_dw(q, _):
        for d in range(2):
            way_copy(q, d).wait_send()
            plain_copy(q, d).wait_send()
            sum_copy(q, d).wait_send()
        return 0

    lax.fori_loop(0, X, done_dw, 0)


def body(student_hidden, head_weight, teacher_logprobs, align_index, align_tiles, grad_scale):
    T, D = student_hidden.shape
    DR, V = head_weight.shape
    VT = teacher_logprobs.shape[1]
    NB = VT // 128
    CG = V // G
    tiles = align_tiles.reshape(align_tiles.shape[0], 256, 128)
    sem = lambda n: pltpu.SemaphoreType.DMA((2, n))
    vm = pltpu.VMEM
    anywhere = pl.BlockSpec(memory_space=pl.ANY)
    in_vmem = pl.BlockSpec(memory_space=pltpu.VMEM)
    hidden_grad, head_grad = pl.pallas_call(
        kernel,
        out_shape=(
            jax.ShapeDtypeStruct((D // Z, T), BF16),
            jax.ShapeDtypeStruct((DR, V), BF16),
        ),
        in_specs=[
            anywhere, anywhere, anywhere,
            pl.BlockSpec(memory_space=pltpu.SMEM),
            anywhere, in_vmem,
        ],
        out_specs=(in_vmem, in_vmem),
        scratch_shapes=[
            vm((T, VT), F32),
            vm((Z, NB, 16, 128), BF16),
            vm((Z * NB, 16, 128), BF16),
            vm((Z * G, 8, 16, 128), BF16),
            vm((Z * G, 8, 16, 128), BF16),
            vm((G, T, D), BF16),
            vm((D, G * T), BF16),
            vm((D, CG), BF16),
            vm((G, T, CG), F32),
            vm((4, 256, 128), BF16),
            vm((G * T, CG), BF16),
            vm((D, CG), F32),
            vm((D, CG), BF16),
            vm((2, X, DR, CG), BF16),
            vm((2, X, DR, CG), BF16),
            vm((2, X, 2, DR, CG), BF16),
            vm((X, C * DR, CG), BF16),
            vm((G, DR, CG), BF16),
            vm((X, T, D), BF16),
            vm((X, T, D), BF16),
            vm((C * T, D), F32),
            vm((X, T, D), BF16),
            vm((X, T, D), BF16),
            vm((Z, T, D // Z), BF16),
            vm((Z, T, D // Z), BF16),
            vm((2, 8, 128), F32),
            vm((G, 2, 8, 128), F32),
            vm((2, 8, 128), F32),
            vm((Z, 2, 8, 128), F32),
            vm((2, 8, 128), F32),
            vm((8, 128), F32),
            vm((Z, 8, 128), F32),
            vm((G, Z, 8, 128), F32),
            vm((8, 128), F32),
            vm((Z, 8, 128), F32),
            vm((8, 128), F32),
            vm((G, 8, 128), F32),
            pltpu.SemaphoreType.DMA((4,)),
            sem(Z), sem(Z * G), sem(X), sem(X), sem(G), sem((Y - 1) * X), sem(G), sem(Z), sem(Z), sem(G), sem(Z), sem(G),
            sem(G), pltpu.SemaphoreType.DMA((2, 6, X)), sem(X), sem(X), sem(Z),
        ],
        compiler_params=pltpu.CompilerParams(
            collective_id=0, has_side_effects=True, vmem_limit_bytes=56 * 2**20
        ),
        name="distill_backward",
    )(
        student_hidden, head_weight, teacher_logprobs, align_index.T, tiles,
        grad_scale.reshape(1, T),
    )
    return hidden_grad.T, head_grad


def solution(mesh):
    placed = (
        P("dp", None),
        P("dp", "vocab"),
        P("dp", "vocab"),
        P(),
        P("vocab", None, None, None),
        P("dp"),
    )
    return jax.shard_map(
        body,
        mesh=mesh,
        in_specs=placed,
        out_specs=(P("dp", "vocab"), P("dp", "vocab")),
        check_vma=False,
    )
```

```python
import jax
import jax.numpy as jnp
from jax import lax
from jax.experimental import pallas as pl
from jax.experimental.pallas import tpu as pltpu
from jax.sharding import PartitionSpec as P

X, Y, C, Z = 4, 4, 2, 8
K = 2
G = X * C
DP = X * Y * C
MESH = pl.DeviceIdType.MESH
F32 = jnp.float32
BF16 = jnp.bfloat16


def to_row(col):
    return jnp.transpose(jnp.broadcast_to(col, (128, 128)))[0:1, :]


def to_cols(row):
    return jnp.transpose(jnp.broadcast_to(row, (128, 128)))


def kernel(
    x_hbm, w_hbm, t_hbm, idx, tiles_hbm, gs_in,
    hg, wg,
    tl, tsend, tall, psend, prcv, x_all, x_t, w_all, e_ref, tiles, dl,
    dwa, dwp, way, way_sum, dwy, dws, dwr, dxp, dsib, dxo, dxs, dxr, hsend, hr,
    st1, st1r, st2, st2r, fin, rs_own, rs_z, rs_all, ms1, ms1r, mg, mg_all,
    sem_l, sem_t, sem_p, sem_x, sem_xf, sem_w, sem_wy, sem_s1, sem_s2, sem_r1, sem_r2, sem_m1, sem_m2,
    sem_dw, sem_dwy, sem_ds, sem_dx, sem_h,
):
    dp = lax.axis_index("dp")
    z = lax.axis_index("vocab")
    x = dp // (Y * C)
    y = (dp // C) % Y
    c = dp % C
    me = x * C + c
    D = x_hbm.shape[1]
    DR = w_hbm.shape[0]
    NB = tl.shape[1] // 128
    CG = w_all.shape[1]

    def dp_of(g):
        return ((g // C) * Y + y) * C + g % C

    sib = (x * Y + y) * C + (1 - c)

    load_t = pltpu.make_async_copy(t_hbm, tl, sem_l.at[0])
    load_t.start()
    load_x = pltpu.make_async_copy(x_hbm, x_all.at[me], sem_l.at[1])
    load_x.start()
    load_w = pltpu.make_async_copy(
        w_hbm.at[:, pl.ds(me * CG, CG)], w_all.at[pl.ds(dp * DR, DR)], sem_l.at[2]
    )
    load_w.start()
    load_tiles = pltpu.make_async_copy(
        tiles_hbm.at[pl.ds(me * 4, 4)], tiles, sem_l.at[3]
    )
    load_tiles.start()

    barrier = pltpu.get_barrier_semaphore()

    def greet_group(i, _):
        g = (me + i % G) % G
        pl.semaphore_signal(
            barrier, inc=1, device_id=(dp_of(g), (z + i // G) % Z), device_id_type=MESH
        )
        return 0

    lax.fori_loop(1, G * Z, greet_group, 0)

    for ry in range(1, Y):
        pl.semaphore_signal(
            barrier,
            inc=1,
            device_id=((x * Y + (y + ry) % Y) * C + c, z),
            device_id_type=MESH,
        )

    load_t.wait()

    def probs(zt, store):
        rows = jnp.exp(tl[pl.ds(zt * 16, 16), :]).astype(BF16)
        for j in range(NB):
            store(j, rows[:, j * 128 : (j + 1) * 128])

    def order(k):
        return 4 + (1 - 2 * (k % 2)) * ((k + 1) // 2)

    def t_copy(rz, src):
        zt = (z + rz) % Z
        return pltpu.make_async_remote_copy(
            src_ref=tsend.at[zt],
            dst_ref=tall.at[pl.ds(src * NB, NB)],
            send_sem=sem_t.at[0, rz],
            recv_sem=sem_t.at[1, rz],
            device_id=(dp, zt),
            device_id_type=MESH,
        )

    def prep(k, _):
        zt = (z + order(k)) % Z

        def store(j, v):
            tsend[zt, j] = v

        probs(zt, store)
        return 0

    lax.fori_loop(0, Z - 1, prep, 0)

    load_tiles.wait()
    ones = jnp.ones((8, 128), BF16)
    for p in range(8):
        tile = tiles[p // 2, (p % 2) * 128 : (p % 2 + 1) * 128, :]
        sums = lax.dot_general(
            ones, tile, (((1,), (1,)), ((), ())), preferred_element_type=F32
        )
        rs_own[p : p + 1, :] = sums[0:1, :]

    pl.semaphore_wait(barrier, (G * Z - 1) + (Y - 1))

    def rz_copy(r, src):
        zt = (z + r) % Z
        return pltpu.make_async_remote_copy(
            src_ref=rs_own,
            dst_ref=rs_z.at[src],
            send_sem=sem_r1.at[0, r],
            recv_sem=sem_r1.at[1, r],
            device_id=(dp, zt),
            device_id_type=MESH,
        )

    def rg_copy(r, src):
        return pltpu.make_async_remote_copy(
            src_ref=rs_z,
            dst_ref=rs_all.at[src],
            send_sem=sem_r2.at[0, r],
            recv_sem=sem_r2.at[1, r],
            device_id=(dp_of((me + r) % G), z),
            device_id_type=MESH,
        )

    def rz_start(r, _):
        rz_copy(r, z).start()
        return 0

    lax.fori_loop(1, Z, rz_start, 0)
    rs_z[z] = rs_own[...]

    def t_start(k, _):
        t_copy(order(k), z).start()
        return 0

    lax.fori_loop(0, Z - 1, t_start, 0)

    def w_copy(r, src_dp):
        g = (me + r) % G
        return pltpu.make_async_remote_copy(
            src_ref=w_hbm.at[:, pl.ds(g * CG, CG)],
            dst_ref=w_all.at[pl.ds(src_dp * DR, DR)],
            send_sem=sem_w.at[0, r],
            recv_sem=sem_w.at[1, r],
            device_id=(dp_of(g), z),
            device_id_type=MESH,
        )

    def w_start(r, _):
        w_copy(r, dp).start()
        return 0

    lax.fori_loop(1, G, w_start, 0)

    def wy_copy(i, back):
        ry = i // X + 1
        xs = i % X
        src_y = (y + Y - ry) % Y if back else y
        rows = pl.ds((xs * Y + src_y) * (C * DR), C * DR)
        return pltpu.make_async_remote_copy(
            src_ref=w_all.at[rows],
            dst_ref=w_all.at[rows],
            send_sem=sem_wy.at[0, i],
            recv_sem=sem_wy.at[1, i],
            device_id=((x * Y + (y + ry) % Y) * C + c, z),
            device_id_type=MESH,
        )

    def x_copy(rx, src_g):
        return pltpu.make_async_remote_copy(
            src_ref=x_hbm,
            dst_ref=x_all.at[src_g],
            send_sem=sem_x.at[0, rx],
            recv_sem=sem_x.at[1, rx],
            device_id=(((x + rx) % X * Y + y) * C + c, z),
            device_id_type=MESH,
        )

    def xs_copy(rx, g, src):
        return pltpu.make_async_remote_copy(
            src_ref=src,
            dst_ref=x_all.at[g],
            send_sem=sem_xf.at[0, rx],
            recv_sem=sem_xf.at[1, rx],
            device_id=(sib, z),
            device_id_type=MESH,
        )

    for rx in (2, 1, 3):
        x_copy(rx, me).start()
    xs_copy(0, me, x_hbm).start()

    def store_own(j, v):
        tall[z * NB + j] = v

    probs(z, store_own)

    def rz_wait(r, _):
        rz_copy(r, (z + Z - r) % Z).wait_recv()
        return 0

    lax.fori_loop(1, Z, rz_wait, 0)
    rs_all[me] = rs_z[...]

    def rg_start(r, _):
        rg_copy(r, me).start()
        return 0

    lax.fori_loop(1, G, rg_start, 0)

    load_w.wait()

    def w_wait(r, _):
        w_copy(r, dp_of((me + G - r) % G)).wait_recv()
        return 0

    lax.fori_loop(1, G, w_wait, 0)

    def wy_start(i, _):
        wy_copy(i, 0).start()
        return 0

    lax.fori_loop(0, (Y - 1) * X, wy_start, 0)

    load_x.wait()
    for rx in (1, 3, 2):
        src = (x + X - rx) % X * C + c
        x_copy(rx, src).wait_recv()
        xs_copy(rx, src, x_all.at[src]).start()

    def group_copy(src, dst, sems, r):
        return pltpu.make_async_remote_copy(
            src_ref=src,
            dst_ref=dst.at[r],
            send_sem=sems.at[0, r],
            recv_sem=sems.at[1, r],
            device_id=(dp_of((me + r) % G), z),
            device_id_type=MESH,
        )

    def z_copy(src, dst, sems, r):
        return pltpu.make_async_remote_copy(
            src_ref=src,
            dst_ref=dst.at[r],
            send_sem=sems.at[0, r],
            recv_sem=sems.at[1, r],
            device_id=(dp, (z + r) % Z),
            device_id_type=MESH,
        )

    def merge(own, came, n, out):
        top = own[0]
        for r in range(1, n):
            top = jnp.maximum(top, came[r, 0])
        total = own[1] * jnp.exp(own[0] - top)
        for r in range(1, n):
            total = total + came[r, 1] * jnp.exp(came[r, 0] - top)
        out[0] = top
        out[1] = total

    def rg_wait(r, _):
        rg_copy(r, (me + G - r) % G).wait_recv()
        return 0

    lax.fori_loop(1, G, rg_wait, 0)

    def t_wait(k, _):
        rz = order(k)
        t_copy(rz, (z + Z - rz) % Z).wait_recv()
        return 0

    lax.fori_loop(0, Z - 1, t_wait, 0)

    def p_copy(i, back):
        sign = 1 - 2 * back
        g = (x + X + sign * (i // 16 + 1)) % X * C + (c + i % 2) % C
        zt = (z + Z + sign * order(i // 2 % 8)) % Z
        return pltpu.make_async_remote_copy(
            src_ref=psend.at[zt * G + g],
            dst_ref=prcv.at[g * Z + zt if back else me * Z + z],
            send_sem=sem_p.at[0, i],
            recv_sem=sem_p.at[1, i],
            device_id=(dp_of(g), zt),
            device_id_type=MESH,
        )

    def weigh(i, acc):
        g = i % G
        zt = i // G
        for p in range(8):
            acc = acc + tall[idx[p % K, i * 4 + p // K]].astype(F32) * rs_all[g, zt, p : p + 1, :]
        return acc

    acc = lax.fori_loop(0, G * Z, weigh, jnp.zeros((16, 128), F32))

    own_mass = jnp.broadcast_to(jnp.sum(acc, axis=1, keepdims=True), (16, 128))
    lane = lax.broadcasted_iota(jnp.int32, (16, 128), 1)
    row = lax.broadcasted_iota(jnp.int32, (16, 128), 0)
    placed = jnp.sum(jnp.where(lane == row + z * 16, own_mass, 0.0), axis=0, keepdims=True)
    ms1[...] = jnp.broadcast_to(placed, (8, 128))

    def mz_start(r, _):
        z_copy(ms1, ms1r, sem_m1, r).start()
        return 0

    lax.fori_loop(1, Z, mz_start, 0)

    SELF = (X - 1) * 16 + 14

    def pick(i, store):
        g = (x + i // 16 + 1) % X * C + (c + i % 2) % C
        zt = (z + order(i // 2 % 8)) % Z
        base = zt * (G * 4) + g * 4
        for p in range(8):
            store(zt * G + g, p, tall[idx[p % K, base + p // K]])

    def pick_send(i, _):
        def store(slot, p, v):
            psend[slot, p] = v

        @pl.when(i != SELF)
        def _():
            pick(i, store)
            p_copy(i, 0).start()

        return 0

    def store_mine(slot, p, v):
        prcv[me * Z + z, p] = v

    lax.fori_loop(0, 16, pick_send, 0)
    pick(SELF, store_mine)

    for rx in range(X):
        xs_copy(rx, (x + X - rx) % X * C + 1 - c, x_hbm).wait_recv()

    def wy_wait(i, _):
        wy_copy(i, 1).wait_recv()
        return 0

    lax.fori_loop(0, (Y - 1) * X, wy_wait, 0)

    def logits(r, _):
        both = jnp.dot(
            x_all[pl.ds(2 * r, 2)].reshape(256, D), w_all[...], preferred_element_type=F32
        )
        for h in range(2):
            l = both[h * 128 : (h + 1) * 128]
            m = jnp.max(l, axis=1, keepdims=True)
            e = jnp.exp(l - m)
            e_ref[2 * r + h] = e
            st1[0, pl.ds(2 * r + h, 1), :] = to_row(m)
            st1[1, pl.ds(2 * r + h, 1), :] = to_row(jnp.sum(e, axis=1, keepdims=True))
        return 0

    lax.fori_loop(0, G // 2, logits, 0)

    def s_start(r, _):
        group_copy(st1, st1r, sem_s1, r).start()
        return 0

    lax.fori_loop(1, G, s_start, 0)


    def mz_wait(r, _):
        z_copy(ms1, ms1r, sem_m1, r).wait_recv()
        return 0

    lax.fori_loop(1, Z, mz_wait, 0)
    mass = ms1[...]
    for r in range(1, Z):
        mass = mass + ms1r[r]
    top_row = lax.broadcasted_iota(jnp.int32, (8, 128), 0) == 0
    mg[...] = jnp.where(top_row, mass, jnp.broadcast_to(gs_in[...], (8, 128)))

    def mg_copy(r, src):
        return pltpu.make_async_remote_copy(
            src_ref=mg,
            dst_ref=mg_all.at[src],
            send_sem=sem_m2.at[0, r],
            recv_sem=sem_m2.at[1, r],
            device_id=(dp_of((me + r) % G), z),
            device_id_type=MESH,
        )

    def mg_start(r, _):
        mg_copy(r, me).start()
        return 0

    lax.fori_loop(1, G, mg_start, 0)
    mg_all[me] = mg[...]

    lax.fori_loop(16, 24, pick_send, 0)

    def x_turn(r, _):
        x_t[:, pl.ds(pl.multiple_of(r * 128, 128), 128)] = jnp.transpose(x_all[r])
        return 0

    lax.fori_loop(0, G, x_turn, 0)

    def s_wait(r, _):
        group_copy(st1, st1r, sem_s1, r).wait_recv()
        return 0

    lax.fori_loop(1, G, s_wait, 0)
    merge(st1, st1r, G, st2)

    def sz_start(r, _):
        z_copy(st2, st2r, sem_s2, r).start()
        return 0

    lax.fori_loop(1, Z, sz_start, 0)
    lax.fori_loop(24, 32, pick_send, 0)


    def sz_wait(r, _):
        z_copy(st2, st2r, sem_s2, r).wait_recv()
        return 0

    lax.fori_loop(1, Z, sz_wait, 0)
    merge(st2, st2r, Z, fin)


    def mg_wait(r, _):
        mg_copy(r, (me + G - r) % G).wait_recv()
        return 0

    lax.fori_loop(1, G, mg_wait, 0)
    for r in range(G):
        st1r[0, 0, r : r + 1, :] = mg_all[r, 0:1, :] * mg_all[r, 1:2, :]
    fin[1] = st1r[0, 0] * jnp.exp(st1[0] - fin[0]) / fin[1]

    NC = D // 512
    PAIR = C * 128

    def ds_copy(k):
        return pltpu.make_async_remote_copy(
            src_ref=dxp.at[k],
            dst_ref=dsib.at[k],
            send_sem=sem_ds.at[0, k],
            recv_sem=sem_ds.at[1, k],
            device_id=(sib, z),
            device_id_type=MESH,
        )

    def dx_copy(k):
        return pltpu.make_async_remote_copy(
            src_ref=dxs.at[k],
            dst_ref=dxr.at[k],
            send_sem=sem_dx.at[0, k],
            recv_sem=sem_dx.at[1, k],
            device_id=(((x + X - k) % X * Y + y) * C + c, z),
            device_id_type=MESH,
        )

    def step_map(s):
        k = (s + 1) % X
        xs = (x + X - k) % X

        def p_wait(i, _):
            @pl.when(s * 16 + i != SELF)
            def _():
                p_copy(s * 16 + i, 1).wait_recv()

            return 0

        lax.fori_loop(0, 16, p_wait, 0)

        @pl.when(s + 2 < X)
        def _():
            lax.fori_loop((s + 2) * 16, (s + 3) * 16, pick_send, 0)

        for cc in range(C):
            r = xs * C + cc
            scale = to_cols(mg_all[r, 1:2, :])
            coef = to_cols(fin[1, pl.ds(r, 1), :])
            for b in range(4):
                first = prcv[pl.ds(r * Z, Z), 2 * b].reshape(128, 128)
                second = prcv[pl.ds(r * Z, Z), 2 * b + 1].reshape(128, 128)
                m = jnp.dot(
                    jnp.concatenate([first, second], axis=1),
                    tiles[b],
                    preferred_element_type=F32,
                )
                cols = slice(b * 128, (b + 1) * 128)
                dl[pl.ds(pl.multiple_of(r * 128, 128), 128), cols] = (
                    coef * e_ref[r, :, cols] - scale * m
                ).astype(BF16)

    def step_dx(s):
        k = (s + 1) % X
        pair = pl.ds(pl.multiple_of((x + X - k) % X * PAIR, PAIR), PAIR)
        for n in range(NC):
            cols = slice(n * 512, (n + 1) * 512)
            dxo[:, cols] = lax.dot_general(
                dl[pair, :], w_all[cols, :], (((1,), (1,)), ((), ())),
                preferred_element_type=F32,
            )
        dxp[k] = dxo[pl.ds(pl.multiple_of((1 - c) * 128, 128), 128), :].astype(BF16)
        ds_copy(k).start()

    def join(k):
        ds_copy(k).wait_recv()
        dxs[k] = (
            dxo[pl.ds(pl.multiple_of(c * 128, 128), 128), :] + dsib[k].astype(F32)
        ).astype(BF16)

    def dw_sums(k, rows):
        pair = pl.ds(pl.multiple_of((x + X - k) % X * PAIR, PAIR), PAIR)
        return jnp.dot(x_t[rows, pair], dl[pair, :], preferred_element_type=F32)

    dwa[...] = jnp.zeros_like(dwa)

    def early(i, _):
        step_map(i)
        step_dx(i)

        def add(q, _):
            rows = pl.ds(pl.multiple_of(q * 384, 384), 384)
            dwa[rows, :] += dw_sums(i + 1, rows)
            return 0

        lax.fori_loop(0, D // 384, add, 0)
        join(i + 1)
        dx_copy(i + 1).start()
        return 0

    lax.fori_loop(0, X - 1, early, 0)

    def done_8(r, _):
        t_copy(r, z).wait_send()
        z_copy(st2, st2r, sem_s2, r).wait_send()
        z_copy(ms1, ms1r, sem_m1, r).wait_send()
        rz_copy(r, z).wait_send()
        group_copy(st1, st1r, sem_s1, r).wait_send()
        rg_copy(r, me).wait_send()
        w_copy(r, dp).wait_send()
        mg_copy(r, me).wait_send()
        return 0

    lax.fori_loop(1, Z, done_8, 0)

    def done_p(i, _):
        @pl.when(i != SELF)
        def _():
            p_copy(i, 0).wait_send()

        return 0

    lax.fori_loop(0, (X - 1) * 16, done_p, 0)
    for rx in range(1, X):
        x_copy(rx, me).wait_send()
    for rx in range(X):
        xs_copy(rx, me, x_hbm).wait_send()

    def done_wy(i, _):
        wy_copy(i, 0).wait_send()
        return 0

    lax.fori_loop(0, (Y - 1) * X, done_wy, 0)
    step_map(X - 1)

    YR = C * DR

    def next_y(d):
        return (y + 1 + d * (Y - 2)) % Y

    def to_y(d):
        return ((x * Y + next_y(d)) * C + c, z)

    def half(q, yt, h):
        return pl.ds((q * Y + yt) * YR + h * DR, DR)

    def way_copy(q, d):
        return pltpu.make_async_remote_copy(
            src_ref=dwp.at[half(q, (y + 2) % Y, d)],
            dst_ref=way.at[d, q],
            send_sem=sem_dwy.at[0, d, q],
            recv_sem=sem_dwy.at[1, d, q],
            device_id=to_y(d),
            device_id_type=MESH,
        )

    def plain_copy(q, d):
        return pltpu.make_async_remote_copy(
            src_ref=dwp.at[half(q, next_y(d), 1 - d)],
            dst_ref=dwy.at[d, q, 1 - d],
            send_sem=sem_dwy.at[0, 2 + d, q],
            recv_sem=sem_dwy.at[1, 2 + d, q],
            device_id=to_y(d),
            device_id_type=MESH,
        )

    def sum_copy(q, d):
        return pltpu.make_async_remote_copy(
            src_ref=way_sum.at[d, q],
            dst_ref=dwy.at[d, q, d],
            send_sem=sem_dwy.at[0, 4 + d, q],
            recv_sem=sem_dwy.at[1, 4 + d, q],
            device_id=to_y(d),
            device_id_type=MESH,
        )

    def dw_part(i):
        q = (x + 1 + i) % X
        rows = pl.ds(pl.multiple_of(q * (Y * YR), Y * YR), Y * YR)
        total = dwa[rows, :] + dw_sums(0, rows)
        dwa[rows, :] = total
        dwp[rows, :] = total.astype(BF16)
        for d in range(2):
            way_copy(q, d).start()
        for d in range(2):
            plain_copy(q, d).start()

    def dw_copy(r, src_g):
        g = (me + r) % G
        return pltpu.make_async_remote_copy(
            src_ref=dws.at[g // C, pl.ds(g % C * DR, DR)],
            dst_ref=dwr.at[src_g],
            send_sem=sem_dw.at[0, r],
            recv_sem=sem_dw.at[1, r],
            device_id=(dp_of(g), z),
            device_id_type=MESH,
        )

    def dw_rest(i, _):
        dw_part(i)
        return 0

    lax.fori_loop(0, 2, dw_rest, 0)
    step_dx(X - 1)
    lax.fori_loop(2, X, dw_rest, 0)

    join(0)

    def dx_wait(k, _):
        dx_copy(k).wait_recv()
        return 0

    lax.fori_loop(1, X, dx_wait, 0)
    for r4 in range(4):
        sub = slice(r4 * 32, (r4 + 1) * 32)
        total = dxs[0, sub, :].astype(F32)
        for k in range(1, X):
            total = total + dxr[k, sub, :].astype(F32)
        for k in range(Z):
            hsend[k, sub, :] = total[:, k * 192 : (k + 1) * 192].astype(BF16)

    def h_copy(r):
        zt = (z + r) % Z
        return pltpu.make_async_remote_copy(
            src_ref=hsend.at[zt],
            dst_ref=hr.at[r],
            send_sem=sem_h.at[0, r],
            recv_sem=sem_h.at[1, r],
            device_id=(dp, zt),
            device_id_type=MESH,
        )

    def h_start(k, _):
        h_copy(order(k)).start()
        return 0

    lax.fori_loop(0, Z - 1, h_start, 0)
    lax.fori_loop((X - 1) * 16, G * Z, done_p, 0)

    def done_dx(k, _):
        dx_copy(k).wait_send()
        ds_copy(k).wait_send()
        return 0

    lax.fori_loop(1, X, done_dx, 0)
    ds_copy(0).wait_send()

    def dw_way(i, _):
        q = (x + 1 + i) % X
        for d in range(2):
            way_copy(q, d).wait_recv()
            way_sum[d, q] = (
                dwa[half(q, next_y(d), d), :] + way[d, q].astype(F32)
            ).astype(BF16)
            sum_copy(q, d).start()
        return 0

    lax.fori_loop(0, X, dw_way, 0)

    def dw_join(i, _):
        q = (x + 1 + i) % X
        for d in range(2):
            plain_copy(q, d).wait_recv()
            sum_copy(q, d).wait_recv()
        for h in range(2):
            total = dwa[half(q, y, h), :]
            for d in range(2):
                total = total + dwy[d, q, h].astype(F32)
            dws[q, h * DR : (h + 1) * DR, :] = total.astype(BF16)
        for cc in range(C):
            r = (q * C + cc + G - me) % G

            @pl.when(r != 0)
            def _():
                dw_copy(r, me).start()

        return 0

    lax.fori_loop(0, X, dw_join, 0)
    dwr[me] = dws[x, pl.ds(pl.multiple_of(c * DR, 16), DR), :]

    def dw_wait(r, _):
        dw_copy(r, (me + G - r) % G).wait_recv()
        return 0

    lax.fori_loop(1, G, dw_wait, 0)
    for g in range(G):
        wg[:, g * CG : (g + 1) * CG] = dwr[g]

    def h_wait(r, _):
        h_copy(r).wait_recv()
        return 0

    lax.fori_loop(1, Z, h_wait, 0)
    total = hsend[z].astype(F32)
    for r in range(1, Z):
        total = total + hr[r].astype(F32)
    hg[...] = jnp.transpose(total).astype(BF16)

    def done_h(r, _):
        h_copy(r).wait_send()
        dw_copy(r, me).wait_send()
        return 0

    lax.fori_loop(1, Z, done_h, 0)

    def done_dw(q, _):
        for d in range(2):
            way_copy(q, d).wait_send()
            plain_copy(q, d).wait_send()
            sum_copy(q, d).wait_send()
        return 0

    lax.fori_loop(0, X, done_dw, 0)


def body(student_hidden, head_weight, teacher_logprobs, align_index, align_tiles, grad_scale):
    T, D = student_hidden.shape
    DR, V = head_weight.shape
    VT = teacher_logprobs.shape[1]
    NB = VT // 128
    CG = V // G
    tiles = align_tiles.reshape(align_tiles.shape[0], 256, 128)
    sem = lambda n: pltpu.SemaphoreType.DMA((2, n))
    vm = pltpu.VMEM
    anywhere = pl.BlockSpec(memory_space=pl.ANY)
    in_vmem = pl.BlockSpec(memory_space=pltpu.VMEM)
    hidden_grad, head_grad = pl.pallas_call(
        kernel,
        out_shape=(
            jax.ShapeDtypeStruct((D // Z, T), BF16),
            jax.ShapeDtypeStruct((DR, V), BF16),
        ),
        in_specs=[
            anywhere, anywhere, anywhere,
            pl.BlockSpec(memory_space=pltpu.SMEM),
            anywhere, in_vmem,
        ],
        out_specs=(in_vmem, in_vmem),
        scratch_shapes=[
            vm((T, VT), F32),
            vm((Z, NB, 16, 128), BF16),
            vm((Z * NB, 16, 128), BF16),
            vm((Z * G, 8, 16, 128), BF16),
            vm((Z * G, 8, 16, 128), BF16),
            vm((G, T, D), BF16),
            vm((D, G * T), BF16),
            vm((D, CG), BF16),
            vm((G, T, CG), F32),
            vm((4, 256, 128), BF16),
            vm((G * T, CG), BF16),
            vm((D, CG), F32),
            vm((D, CG), BF16),
            vm((2, X, DR, CG), BF16),
            vm((2, X, DR, CG), BF16),
            vm((2, X, 2, DR, CG), BF16),
            vm((X, C * DR, CG), BF16),
            vm((G, DR, CG), BF16),
            vm((X, T, D), BF16),
            vm((X, T, D), BF16),
            vm((C * T, D), F32),
            vm((X, T, D), BF16),
            vm((X, T, D), BF16),
            vm((Z, T, D // Z), BF16),
            vm((Z, T, D // Z), BF16),
            vm((2, 8, 128), F32),
            vm((G, 2, 8, 128), F32),
            vm((2, 8, 128), F32),
            vm((Z, 2, 8, 128), F32),
            vm((2, 8, 128), F32),
            vm((8, 128), F32),
            vm((Z, 8, 128), F32),
            vm((G, Z, 8, 128), F32),
            vm((8, 128), F32),
            vm((Z, 8, 128), F32),
            vm((8, 128), F32),
            vm((G, 8, 128), F32),
            pltpu.SemaphoreType.DMA((4,)),
            sem(Z), sem(Z * G), sem(X), sem(X), sem(G), sem((Y - 1) * X), sem(G), sem(Z), sem(Z), sem(G), sem(Z), sem(G),
            sem(G), pltpu.SemaphoreType.DMA((2, 6, X)), sem(X), sem(X), sem(Z),
        ],
        compiler_params=pltpu.CompilerParams(
            collective_id=0, has_side_effects=True, vmem_limit_bytes=56 * 2**20
        ),
        name="distill_backward",
    )(
        student_hidden, head_weight, teacher_logprobs, align_index.T, tiles,
        grad_scale.reshape(1, T),
    )
    return hidden_grad.T, head_grad


def solution(mesh):
    placed = (
        P("dp", None),
        P("dp", "vocab"),
        P("dp", "vocab"),
        P(),
        P("vocab", None, None, None),
        P("dp"),
    )
    return jax.shard_map(
        body,
        mesh=mesh,
        in_specs=placed,
        out_specs=(P("dp", "vocab"), P("dp", "vocab")),
        check_vma=False,
    )
```
